256 devices in a mesh: tile: 64 (over z, y, core), lev: 4 (over x).
Axes of the slice: x: 4, y: 4, z: 8, core: 2. Of those that a mesh axis runs over, the one named last changes fastest.
Arguments:
- control: float32 [20, 1024, 4352], P('lev', 'tile'), may hold values from -6 to 6
- land_sea: int32 [1024, 4352], P('tile'), may hold values 0 or 1
- diffusivity: float32 [1024, 4352], P('tile'), may hold values from 0.22 to 0.245
- profile_counts: int32 [64], P('tile'), may hold values from 256 to 512, as said below
- owner_tile: int32 [32768, 1], P('tile'), may hold values from 0 to 63; in each aligned block of 512 rows (0 to 511, 512 to 1023, ...) at most 12 rows name the same one
- stencil_cells: int32 [32768, 4], P('tile'), may hold values from 0 to 69631
- stencil_weights: float32 [32768, 4], P('tile'), may hold values from 0.1 to 1
- inverse_error: float32 [32768, 20], P('tile', 'lev'), may hold values from 0.8 to 5
- correlation_inverse: float32 [20, 20], replicated, as said below
Outputs:
- product: float32 [20, 1024, 4352], P('lev', 'tile')
The draws below stay inside these ranges and needn't reach their ends.
Inputs may be any that keep to these rules, and one draw needn't show every extreme that they name: `profile_counts`: every value lies between 256 and 512, and one block has all 512 slots live. `owner_tile`: among the 512 rows of one storage block no tile is named more than 12 times. `correlation_inverse`: symmetric.
All inputs are finite; a program needn't handle non-finite values. No bound on the sum of `land_sea` on one device may be relied on, other than what follows from the above.
Results may differ from the reference program's by a relative error of at most 0.00005.
Values sent between devices are 32-bit elements; how exact they have to be, the bound alone decides.
A program may use at most 128 MiB of HBM per device.

```python
import math
import jax
import jax.numpy as jnp
import numpy as np
from jax import lax

CX = 16
NY = 4352
ITERS = 10
P_DEV = 512
NX = 1024
LEV = 20
PROFILES = 32768
CAP = 12
N_TILE = 64


def draw_profile_counts(key, part):
    count_key, pick_key = jax.random.split(key)
    counts = jax.random.randint(count_key, (N_TILE,), P_DEV // 2, P_DEV + 1)
    chosen = jax.random.randint(pick_key, (), 0, N_TILE)
    return jnp.where(jnp.arange(N_TILE) == chosen, P_DEV, counts).astype(jnp.int32)


def draw_stencil_cells(key, part):
    key = jax.random.fold_in(key, 7)
    rim_key, any_key, mix_key, col_key = jax.random.split(key, 4)
    rim_pick = jax.random.randint(rim_key, (PROFILES, 4), 0, 4)
    rim_rows = jnp.where(rim_pick < 2, rim_pick, CX - 4 + rim_pick)
    any_rows = jax.random.randint(any_key, (PROFILES, 4), 0, CX)
    mixing = jax.random.randint(mix_key, (PROFILES, 4), 0, 4)
    rows = jnp.where(mixing == 0, any_rows, rim_rows)
    columns = jax.random.randint(col_key, (PROFILES, 4), 0, NY)
    cells = rows * NY + columns
    first_row = jnp.arange(PROFILES)[:, None] == 0
    entry = jnp.arange(4)[None, :]
    cells = jnp.where(first_row & (entry == 0), 0, cells)
    cells = jnp.where(first_row & (entry == 1), CX * NY - 1, cells)
    return cells.astype(jnp.int32)


def draw_correlation_inverse(key, part):
    ratio_key, noise_key = jax.random.split(key)
    decay_ratio = jax.random.uniform(ratio_key, (), jnp.float32, 0.55, 0.75)
    far_noise = jax.random.uniform(noise_key, (LEV, LEV), jnp.float32, -1.0, 1.0)
    row_index = jnp.arange(LEV)[:, None]
    col_index = jnp.arange(LEV)[None, :]
    distance = jnp.abs(row_index - col_index)
    kac_scale = 1.0 / (1.0 - decay_ratio * decay_ratio)
    end_rows = ((row_index == 0) | (row_index == LEV - 1)).astype(jnp.float32)
    diagonal = kac_scale * (1.0 + decay_ratio * decay_ratio * (1.0 - end_rows))
    tridiagonal = jnp.where(distance == 0, diagonal, jnp.where(distance == 1, -decay_ratio * kac_scale, 0.0))
    far_entries = jnp.where(distance >= 2, 0.01 * (far_noise + jnp.transpose(far_noise)), 0.0)
    return (tridiagonal + far_entries).astype(jnp.float32)


def place_ends(entries, key, smallest, high):
    spot = [jax.random.randint(jax.random.fold_in(key, axis), (), 0, length) for axis, length in enumerate(entries.shape)]
    longest = entries.shape.index(max(entries.shape))
    beside = spot[:longest] + [(spot[longest] + 1) % entries.shape[longest]] + spot[longest + 1:]
    return entries.at[tuple(spot)].set(smallest).at[tuple(beside)].set(high)


def shard_levels(own_key, shape, cuts, least, high):
    level = 1.0
    for position, parts in cuts:
        heights = jax.random.uniform(jax.random.fold_in(jax.random.fold_in(own_key, 6), position), (parts,), jnp.float32, least / len(cuts), high / len(cuts))
        level = level * jnp.repeat(jnp.exp(heights), shape[position] // parts).reshape((-1,) + (1,) * (len(shape) - 1 - position))
    return level


def shared_out(own_key, own, number, rows, amount, top, bound, lean):
    ranking = jax.random.permutation(own_key, amount)
    crowded, ordinary = shares(amount, rows * top, bound, lean, True), shares(amount, rows * top, bound, lean, False)
    places = jnp.arange(amount)

    def named(tallies, turn):
        used = int((tallies > 0).sum())
        fixed = max(1, used // 4)
        shifted = fixed + (places - fixed + turn * (used - fixed)) % max(1, amount - fixed)
        return jnp.zeros((amount,), jnp.int32).at[ranking[jnp.where(places < fixed, places, shifted)]].set(jnp.asarray(tallies, jnp.int32))

    tallies = jnp.where(number % 4 == 0, named(crowded, number // 4), named(ordinary, number - number // 4 - 1))
    mixed = jax.random.permutation(jax.random.fold_in(own, 3), amount)
    source_of, receiver = mixed[0:amount // 2 * 2:2], mixed[1:amount // 2 * 2:2]
    slack = jnp.minimum(tallies[source_of] - 1, bound - tallies[receiver]) // 2
    slack = jnp.where((source_of == ranking[0]) | (receiver == ranking[0]) | (tallies[receiver] == 0), 0, jnp.maximum(slack, 0))
    shifted = jax.random.randint(jax.random.fold_in(own, 4), (amount // 2,), 0, 1 << 20) % (slack + 1)
    tallies = tallies.at[source_of].add(-shifted).at[receiver].add(shifted)
    members = jnp.searchsorted(jnp.cumsum(tallies), jnp.arange(rows * top), side="right").astype(jnp.int32)
    listing = members.reshape(top, rows).T
    listing = listing[jax.random.permutation(jax.random.fold_in(own, 1), rows)]
    turn = jax.random.randint(jax.random.fold_in(own, 2), (rows, 1), 0, top)
    return jnp.take_along_axis(listing, (jnp.arange(top)[None, :] + turn) % top, axis=1)


def shares(count, total, reach, lean, full):
    portions = [(1 << 20) // math.isqrt(grade ** lean) + 1 for grade in range(1, count + 1)]
    largest = reach if full else min(reach, max(-(-total // count), total * portions[0] // sum(portions)))
    least = 1 if total - largest >= count - 1 else 0
    given, surplus = [largest] + [least] * (count - 1), total - largest - least * (count - 1)
    while surplus > 0:
        candidates = [i for i in range(1, count) if given[i] < largest] or [i for i in range(1, count) if given[i] < reach]
        mass, remaining = sum([portions[i] for i in candidates]), surplus
        for i in candidates:
            more = min(reach - given[i], max(1, remaining * portions[i] // mass), surplus)
            given[i] = given[i] + more
            surplus = surplus - more
    return np.array(given)


def centred(stream_key, dims, scale, reach, shards=(), kind=jnp.bfloat16):
    result = jax.random.normal(stream_key, dims, jnp.float32) * scale
    if len(shards) > 0:
        result = shard_levels(stream_key, dims, shards, -0.22, 0.18) * result
    return jnp.clip(result, min=-reach, max=reach).astype(kind)


def setup_inputs(seed: int = 0) -> dict:
    key_list = jax.random.split(jax.random.key(seed), 10)
    control = centred(key_list[0], (LEV, NX, NY), 1.0, 6.0, ((0, 4), (1, 64)), jnp.float32)
    land_sea = place_ends((jax.random.randint(key_list[1], (NX, NY), 0, 25) < 24).astype(jnp.int32), jax.random.fold_in(key_list[1], 1), 0, 1)
    diffusivity = jnp.clip(jnp.exp(math.log(0.245) - 0.10763069 * jax.random.uniform(key_list[2], (NX, NY), jnp.float32) ** shard_levels(key_list[2], (NX, NY), ((0, 64),), -0.2, 0.2)), 0.22, 0.245)
    profile_counts = draw_profile_counts(jax.random.fold_in(key_list[9], 71), 0)
    owner_tile_keys = jax.random.split(jax.random.fold_in(key_list[4], 1), PROFILES // P_DEV)
    owner_tile_turns = jax.random.permutation(jax.random.fold_in(key_list[4], 3), PROFILES // P_DEV)
    owner_tile = jax.vmap(lambda own, number: shared_out(jax.random.fold_in(key_list[4], 2), own, number, P_DEV, N_TILE, 1, CAP, 2))(owner_tile_keys, owner_tile_turns).reshape((PROFILES, 1))
    stencil_cells = draw_stencil_cells(jax.random.fold_in(key_list[9], 71), 0)
    stencil_weights = jnp.clip(0.1 + 0.9 * jax.random.uniform(key_list[6], (PROFILES, 4), jnp.float32) ** shard_levels(key_list[6], (PROFILES, 4), ((0, 64),), -0.2, 0.2), 0.1, 1.0)
    inverse_error = jnp.clip(jnp.exp(math.log(5.0) - 1.8325814 * jax.random.uniform(key_list[7], (PROFILES, LEV), jnp.float32) ** shard_levels(key_list[7], (PROFILES, LEV), ((0, 64), (1, 4)), -0.2, 0.2)), 0.8, 5.0)
    correlation_inverse = draw_correlation_inverse(jax.random.fold_in(key_list[9], 71), 0)
    return {"control": control, "land_sea": land_sea, "diffusivity": diffusivity, "profile_counts": profile_counts, "owner_tile": owner_tile, "stencil_cells": stencil_cells, "stencil_weights": stencil_weights, "inverse_error": inverse_error, "correlation_inverse": correlation_inverse}


def diffuse(values, edge_rows, edge_cols):
    for counter in range(ITERS):
        flux_rows = edge_rows * (values[:, 1:] - values[:, :-1])
        flux_rows = jnp.pad(flux_rows, ((0, 0), (1, 1), (0, 0)))
        flux_cols = edge_cols * (values[:, :, 1:] - values[:, :, :-1])
        flux_cols = jnp.pad(flux_cols, ((0, 0), (0, 0), (1, 1)))
        values = values + (flux_rows[:, 1:] - flux_rows[:, :-1]) + (flux_cols[:, :, 1:] - flux_cols[:, :, :-1])
    return values

def reference(control, land_sea, diffusivity, profile_counts, owner_tile, stencil_cells, stencil_weights, inverse_error, correlation_inverse):
    ocean_mask = land_sea.astype(jnp.float32)
    half_edge = jnp.sqrt(ocean_mask * diffusivity)
    edge_rows = half_edge[1:] * half_edge[:-1]
    edge_cols = half_edge[:, 1:] * half_edge[:, :-1]
    background = diffuse(control * ocean_mask[None], edge_rows, edge_cols)
    flattened = background.reshape(LEV, NX * NY)
    global_cell = (owner_tile[:, 0:1].astype(jnp.int32) * (CX * NY) + stencil_cells.astype(jnp.int32)).reshape(PROFILES * 4)
    profile_index = jnp.arange(PROFILES, dtype=jnp.int32)
    storer = profile_index // P_DEV
    living = (profile_index % P_DEV < profile_counts[storer]).astype(jnp.float32)
    weights = stencil_weights * living[:, None]
    picked = flattened[:, global_cell].reshape(LEV, PROFILES, 4)
    modeled = lax.optimization_barrier(jnp.sum(picked * weights[None], axis=2))
    scaled = modeled * jnp.transpose(inverse_error)
    coupled = jnp.dot(correlation_inverse, scaled, precision=lax.Precision.HIGHEST, preferred_element_type=jnp.float32)
    weighted = jnp.transpose(inverse_error) * coupled
    spread = (weighted[:, :, None] * weights[None]).reshape(LEV, PROFILES * 4)
    adjoint = jnp.zeros((LEV, NX * NY), jnp.float32).at[:, global_cell].add(spread)
    returned = diffuse(adjoint.reshape(LEV, NX, NY), edge_rows, edge_cols)
    return control + returned * ocean_mask[None]
```

```python
import functools

import jax
import jax.numpy as jnp
from jax import lax
from jax.experimental import pallas as pl
from jax.experimental.pallas import tpu as pltpu
from jax.sharding import PartitionSpec as P

ITERS = 10
DEPTH = ITERS
NEAR = 5
SRC = 64
RANKS = 12
F32, BF16 = jnp.float32, jnp.bfloat16
NT = (((1,), (1,)), ((), ()))


def up_to(n, m):
    return -(-n // m) * m


def kernel(dims, ctrl, land, diff, owner, cells, weights, errors, counts, corr, out,
           u, hb, ca, cb, rh, sbuf, rbuf, wk, ln, er, acc, oh, vf, vt, sv, xt, adj, sb,
           halo_send, halo_recv, prof_send, prof_recv, lev_send, lev_recv):
    tiles, levs, n_l, height, n_t, stored = dims
    pitch, body, front = n_t + 1, up_to((n_t + 1) * n_l, 8), 8
    hw = up_to(n_t, 8)
    qn, qp = height * n_t, up_to(height * n_t, 128)
    slots = RANKS * SRC
    tile, lev = lax.axis_index("tile"), lax.axis_index("lev")
    lane = lax.broadcasted_iota(jnp.int32, (1, 128), 1)
    first, last = lane == 0, lane == 127

    barrier = pltpu.get_barrier_semaphore()

    def greet(i, carry):
        pl.semaphore_signal(barrier, inc=1, device_id={"tile": lax.rem(tile + i, tiles)})
        return carry

    lax.fori_loop(1, tiles, greet, 0)
    for i in range(1, levs):
        pl.semaphore_signal(barrier, inc=1, device_id={"lev": lax.rem(lev + i, levs)})

    rows_all = height + 2 * DEPTH

    def clear(r, carry):
        for slot in range(4):
            u[slot, r, 0:front, :] = jnp.zeros((front, 128), F32)
            u[slot, r, front + body:front + body + 8, :] = jnp.zeros((8, 128), F32)
        hb[r, 0:8, :] = jnp.zeros((8, 128), F32)
        hb[r, 8 + hw:16 + hw, :] = jnp.zeros((8, 128), F32)
        return carry

    lax.fori_loop(0, rows_all, clear, 0)

    def clear_halo(lo):
        def one(r, carry):
            for slot in (0, 3):
                u[slot, r, front:front + body, :] = jnp.zeros((body, 128), F32)
            hb[r, 8:8 + hw, :] = jnp.zeros((hw, 128), F32)
            return carry

        lax.fori_loop(lo, lo + DEPTH, one, 0)

    @pl.when(tile == 0)
    def _():
        clear_halo(0)

    @pl.when(tile == tiles - 1)
    def _():
        clear_halo(DEPTH + height)

    for r in range(height):
        part, sub = r // 8, r % 8
        here = pl.ds(sub, n_t, stride=8)
        h = jnp.sqrt(land[part, here, :].astype(F32) * diff[part, here, :])
        hb[DEPTH + r, hw:8 + hw, :] = jnp.zeros((8, 128), F32)
        hb[DEPTH + r, 8:8 + n_t, :] = h
        rh[r, 0:n_t, :] = jnp.where(h > 0, 1.0 / h, 0.0)
        for l in range(n_l):
            at = front + pitch * l
            u[0, DEPTH + r, at:at + n_t, :] = h * ctrl[l, part, here, :]
            for slot in (0, 3):
                end = at + pitch if l < n_l - 1 else front + body
                u[slot, DEPTH + r, at + n_t:end, :] = jnp.zeros((end - at - n_t, 128), F32)

    spot = lax.broadcasted_iota(jnp.int32, (1, stored), 1)
    living = spot < counts[0]
    is_owner = jnp.where(
        (lax.broadcasted_iota(jnp.int32, (SRC, stored), 0) == owner[...]) & living, 1.0, 0.0
    )
    mine = is_owner.astype(BF16)
    before = jnp.where(
        lax.broadcasted_iota(jnp.int32, (stored, stored), 0)
        < lax.broadcasted_iota(jnp.int32, (stored, stored), 1), 1.0, 0.0
    ).astype(BF16)
    ahead = jnp.dot(mine, before, preferred_element_type=F32)
    rank = jnp.sum(ahead * is_owner, axis=0, keepdims=True)
    data = jnp.concatenate(
        [cells[...].astype(F32), weights[...], errors[...], jnp.zeros((8 - n_l, stored), F32)], axis=0
    )
    spread_out = jnp.concatenate([jnp.where(rank == float(r), data, 0.0) for r in range(16)], axis=0)
    message = jnp.zeros((SRC, 256), F32)
    left = spread_out
    for _ in range(3):
        piece = left.astype(BF16)
        message += lax.dot_general(mine, piece, NT, preferred_element_type=F32)
        left = left - piece.astype(F32)
    sbuf[...] = message.reshape(SRC, 1, 256)

    pl.semaphore_wait(barrier, tiles - 1 + levs - 1)

    def halo(which, side, chunk, root=False):
        lo, n = (0, NEAR) if chunk == 0 else (NEAR, DEPTH - NEAR)
        if side == 0:
            src, dst = DEPTH + lo, DEPTH + height + lo
        else:
            src, dst = height + DEPTH - lo - n, DEPTH - lo - n
        if root:
            a, b, which = hb.at[pl.ds(src, n), pl.ds(8, hw)], hb.at[pl.ds(dst, n), pl.ds(8, hw)], 2
        else:
            slot = 3 * which
            a = u.at[slot, pl.ds(src, n), pl.ds(front, body)]
            b = u.at[slot, pl.ds(dst, n), pl.ds(front, body)]
        return pltpu.make_async_remote_copy(
            src_ref=a, dst_ref=b, send_sem=halo_send.at[which, side, chunk], recv_sem=halo_recv.at[which, side, chunk],
            device_id={"tile": lax.rem(tile + (tiles - 1 if side == 0 else 1), tiles)},
        )

    def has(side):
        return tile > 0 if side == 0 else tile < tiles - 1

    def start_halo(which, chunk, root=False):
        for side in (0, 1):
            @pl.when(has(side))
            def _():
                halo(which, side, chunk, root).start()

    def wait_halo(which, chunk, root=False):
        for side in (0, 1):
            @pl.when(has(1 - side))
            def _():
                halo(which, side, chunk, root).wait_recv()

    def wait_sent(which, chunk, root=False):
        for side in (0, 1):
            @pl.when(has(side))
            def _():
                halo(which, side, chunk, root).wait_send()

    for chunk in (0, 1):
        start_halo(0, chunk, root=True)
        start_halo(0, chunk)

    def profile_copy(to, frm):
        return pltpu.make_async_remote_copy(
            src_ref=sbuf.at[to], dst_ref=rbuf.at[tile], send_sem=prof_send.at[to], recv_sem=prof_recv.at[frm],
            device_id={"tile": to},
        )

    def send_profiles(i, carry):
        to = lax.rem(tile + i, tiles)
        profile_copy(to, tile).start()
        return carry

    lax.fori_loop(1, tiles, send_profiles, 0)
    own = pltpu.make_async_copy(sbuf.at[tile], rbuf.at[tile], prof_recv.at[tile])
    own.start()

    def coefficients(lo, hi):
        def one(r, carry):
            h = hb[r, 8:8 + n_t, :]
            west = pltpu.roll(jnp.where(last, hb[r, 7:7 + n_t, :], h), 1, 1)
            east = pltpu.roll(jnp.where(first, hb[r, 9:9 + n_t, :], h), 127, 1)
            a = 1.0 - h * ((hb[r - 1, 8:8 + n_t, :] + hb[r + 1, 8:8 + n_t, :]) + (west + east))
            b = h * h
            for l in range(n_l):
                at = front + pitch * l
                end = at + pitch if l < n_l - 1 else front + body
                ca[r, at:at + n_t, :] = a
                cb[r, at:at + n_t, :] = b
                ca[r, at + n_t:end, :] = jnp.zeros((end - at - n_t, 128), F32)
                cb[r, at + n_t:end, :] = jnp.zeros((end - at - n_t, 128), F32)
            return carry

        lax.fori_loop(lo, hi, one, 0)

    def sweep(base, s, lo, hi):
        src, dst = jnp.where(s == 1, base, 1 + lax.rem(s, 2)), 1 + lax.rem(s + 1, 2)

        def one(r, carry):
            for j in range(front, front + body, 8):
                here = pl.ds(j, 8)
                c = u[src, r, here, :]
                west = pltpu.roll(jnp.where(last, u[src, r, j - 1:j + 7, :], c), 1, 1)
                east = pltpu.roll(jnp.where(first, u[src, r, j + 1:j + 9, :], c), 127, 1)
                around = (u[src, r - 1, here, :] + u[src, r + 1, here, :]) + (west + east)
                u[dst, r, here, :] = ca[r, here, :] * c + cb[r, here, :] * around
            return carry

        lax.fori_loop(lo + DEPTH, hi + DEPTH, one, 0)

    mid = height // 2

    def inner(base):
        def one(s, carry):
            sweep(base, s, s, height - s)
            return carry

        lax.fori_loop(1, mid, one, 0)

    def outer(base, old, new):
        def one(s, carry):
            sweep(base, s, s - new, jnp.minimum(s - old, mid))
            sweep(base, s, jnp.maximum(height - s + old, mid), height - s + new)
            return carry

        lax.fori_loop(1, ITERS + 1, one, 0)

    coefficients(DEPTH + 1, DEPTH + height - 1)
    inner(0)

    def got_profile(i, carry):
        frm = lax.rem(tile + i, tiles)
        profile_copy(frm, frm).wait_recv()
        return carry

    lax.fori_loop(1, tiles, got_profile, 0)
    own.wait()
    heard = jnp.concatenate([rbuf[...].reshape(SRC, 256), jnp.zeros((128 - SRC, 256), F32)], axis=0)
    turned = jnp.transpose(heard)
    for pair in range(RANKS // 2):
        both = turned[32 * pair:32 * pair + 16] + pltpu.roll(turned[32 * pair + 16:32 * pair + 32], SRC, 1)
        for k in range(4):
            where = pl.ds(k * slots + pair * 128, 128)
            cell = both[k:k + 1].astype(jnp.int32)
            wk[1:2, where] = (cell >> 7).astype(F32)
            ln[0:1, where] = cell & 127
            wk[0:1, where] = both[4 + k:5 + k]
        er[0:8, pl.ds(pair * 128, 128)] = both[8:16]

    def one_hots(i, carry):
        rows = lax.broadcasted_iota(jnp.int32, (128, 4 * slots), 0) + i * 128
        hot = jnp.where(rows == wk[1:2, :].astype(jnp.int32), 1.0, 0.0).astype(BF16)
        oh[pl.ds(pl.multiple_of(i * 128, 128), 128), :] = hot
        oh[pl.ds(pl.multiple_of(qp + i * 128, 128), 128), :] = hot
        return carry

    lax.fori_loop(0, qp // 128, one_hots, 0)

    wait_halo(0, 0, root=True)
    coefficients(DEPTH - NEAR + 1, DEPTH + 1)
    coefficients(DEPTH + height - 1, DEPTH + height + NEAR - 1)
    wait_halo(0, 0)
    outer(0, 0, NEAR)
    wait_halo(0, 1, root=True)
    coefficients(1, DEPTH - NEAR + 1)
    coefficients(DEPTH + height + NEAR - 1, rows_all - 1)
    wait_halo(0, 1)
    for chunk in (0, 1):
        wait_sent(0, chunk, root=True)
        wait_sent(0, chunk)
    outer(0, NEAR, DEPTH)

    for l in range(n_l):
        at = front + pitch * l
        for r in range(height):
            vf[l, r * n_t:(r + 1) * n_t, :] = rh[r, 0:n_t, :] * u[2, DEPTH + r, at:at + n_t, :]
        if qp > qn:
            vf[l, qn:qp, :] = jnp.zeros((qp - qn, 128), F32)

    def turn(l, carry):
        here = pl.ds(pl.multiple_of(l * 128, 128), 128)
        value = jnp.transpose(vf[l, :, :])
        high = value.astype(BF16)
        vt[here, 0:qp] = high
        vt[here, qp:2 * qp] = (value - high.astype(F32)).astype(BF16)
        return carry

    lax.fori_loop(0, n_l, turn, 0)
    acc[...] = jnp.zeros_like(acc)
    split = slots // 256

    def pick(i, carry):
        where = pl.ds(pl.multiple_of(i * 256, 256), 256)
        into = pl.ds(pl.multiple_of(lax.rem(i, split) * 256, 256), 256)
        got = jnp.dot(vt[...], oh[:, where], preferred_element_type=F32)
        on = lax.broadcasted_iota(jnp.int32, (128, 256), 0) == ln[0:1, where]
        weight = wk[0:1, where]
        for l in range(n_l):
            value = jnp.where(on, got[l * 128:(l + 1) * 128], 0.0).reshape(16, 8, 256)
            acc[l, :, into] += jnp.sum(value, axis=0) * weight
        return carry

    lax.fori_loop(0, 4 * split, pick, 0)
    sb[lev, :, :] = jnp.zeros((8, slots), F32)
    for l in range(n_l):
        sb[lev, l:l + 1, :] = jnp.sum(acc[l], axis=0, keepdims=True) * er[l:l + 1, :]

    def level_copy(i, back=False):
        other = lax.rem(lev + (levs - i if back else i), levs)
        return pltpu.make_async_remote_copy(
            src_ref=sb.at[lev], dst_ref=sb.at[other if back else lev], send_sem=lev_send.at[other],
            recv_sem=lev_recv.at[other if back else lev], device_id={"lev": other},
        )

    for i in range(1, levs):
        level_copy(i).start()
    for i in range(1, levs):
        level_copy(i, back=True).wait_recv()
    coupled = [jnp.zeros((1, slots), F32) for _ in range(n_l)]
    for m in range(levs):
        for j in range(n_l):
            row = sb[m, j:j + 1, :]
            for l in range(n_l):
                coupled[l] = coupled[l] + corr[n_l * lev + l, n_l * m + j] * row
    for l in range(n_l):
        weighted = coupled[l] * er[l:l + 1, :]
        for k in range(4):
            where = pl.ds(k * slots, slots)
            value = weighted * wk[0:1, where]
            high = value.astype(BF16).astype(F32)
            sv[l, 0:1, where] = high
            sv[n_l + l, 0:1, where] = value - high

    def put(i, carry):
        rows = lax.broadcasted_iota(jnp.int32, (128, 4 * slots), 0)
        on = rows == ln[0:1, :]
        for g in range(2):
            xt[g * 128:(g + 1) * 128, :] = jnp.where(on, sv[2 * i + g, 0:1, :], 0.0).astype(BF16)
        adj[i, 0:qn, :] = lax.dot_general(oh[0:qn, :], xt[...], NT, preferred_element_type=F32)
        return carry

    lax.fori_loop(0, n_l, put, 0)
    for r in range(height):
        h = hb[DEPTH + r, 8:8 + n_t, :]
        for l in range(n_l):
            at = front + pitch * l
            low = n_l + l
            both = (
                adj[l // 2, r * n_t:(r + 1) * n_t, (l % 2) * 128:(l % 2 + 1) * 128]
                + adj[low // 2, r * n_t:(r + 1) * n_t, (low % 2) * 128:(low % 2 + 1) * 128]
            )
            u[3, DEPTH + r, at:at + n_t, :] = h * both

    for chunk in (0, 1):
        start_halo(1, chunk)
    inner(3)
    wait_halo(1, 0)
    outer(3, 0, NEAR)
    wait_halo(1, 1)
    for chunk in (0, 1):
        wait_sent(1, chunk)
    outer(3, NEAR, DEPTH)

    for r in range(height):
        part, here = r // 8, pl.ds(r % 8, n_t, stride=8)
        for l in range(n_l):
            at = front + pitch * l
            out[l, part, here, :] = rh[r, 0:n_t, :] * u[2, DEPTH + r, at:at + n_t, :]

    def sent_profile(i, carry):
        profile_copy(lax.rem(tile + i, tiles), tile).wait_send()
        return carry

    lax.fori_loop(1, tiles, sent_profile, 0)
    for i in range(1, levs):
        level_copy(i).wait_send()


def tiled(x, height, n_t):
    lead = x.shape[:-2]
    n = len(lead)
    x = x.reshape(lead + (height // 8, 8, n_t, 128))
    x = jnp.swapaxes(x, n + 1, n + 2)
    return x.reshape(lead + (height // 8, n_t * 8, 128))


def untiled(x, height, n_t):
    lead = x.shape[:-3]
    n = len(lead)
    x = x.reshape(lead + (height // 8, n_t, 8, 128))
    x = jnp.swapaxes(x, n + 1, n + 2)
    return x.reshape(lead + (height, n_t * 128))


def per_device(dims, control, land_sea, diffusivity, profile_counts, owner_tile, stencil_cells, stencil_weights,
               inverse_error, correlation_inverse):
    tiles, levs, n_l, height, n_t, stored = dims
    body = up_to((n_t + 1) * n_l, 8)
    hw = up_to(n_t, 8)
    rows = height + 2 * DEPTH
    qn, qp = height * n_t, up_to(height * n_t, 128)
    slots = RANKS * SRC
    vmem = pl.BlockSpec(memory_space=pltpu.VMEM)
    smem = pl.BlockSpec(memory_space=pltpu.SMEM)
    returned = pl.pallas_call(
        functools.partial(kernel, dims),
        out_shape=jax.ShapeDtypeStruct((n_l, height // 8, n_t * 8, 128), F32),
        in_specs=[vmem] * 7 + [smem] * 2,
        out_specs=vmem,
        scratch_shapes=[
            pltpu.VMEM((4, rows, body + 16, 128), F32),
            pltpu.VMEM((rows, hw + 16, 128), F32),
            pltpu.VMEM((rows, body + 16, 128), F32),
            pltpu.VMEM((rows, body + 16, 128), F32),
            pltpu.VMEM((height, hw, 128), F32),
            pltpu.VMEM((SRC, 1, 256), F32),
            pltpu.VMEM((SRC, 1, 256), F32),
            pltpu.VMEM((2, 4 * slots), F32),
            pltpu.VMEM((1, 4 * slots), jnp.int32),
            pltpu.VMEM((8, slots), F32),
            pltpu.VMEM((n_l, 8, slots), F32),
            pltpu.VMEM((2 * qp, 4 * slots), BF16),
            pltpu.VMEM((n_l, qp, 128), F32),
            pltpu.VMEM((n_l * 128, 2 * qp), BF16),
            pltpu.VMEM((2 * n_l, 1, 4 * slots), F32),
            pltpu.VMEM((256, 4 * slots), BF16),
            pltpu.VMEM((n_l, up_to(qn, 8), 256), F32),
            pltpu.VMEM((levs, 8, slots), F32),
            pltpu.SemaphoreType.DMA((3, 2, 2)),
            pltpu.SemaphoreType.DMA((3, 2, 2)),
            pltpu.SemaphoreType.DMA((SRC,)),
            pltpu.SemaphoreType.DMA((SRC,)),
            pltpu.SemaphoreType.DMA((levs,)),
            pltpu.SemaphoreType.DMA((levs,)),
        ],
        compiler_params=pltpu.CompilerParams(
            collective_id=0, has_side_effects=True, vmem_limit_bytes=60 * 2**20
        ),
    )(
        tiled(control, height, n_t),
        tiled(land_sea, height, n_t),
        tiled(diffusivity, height, n_t),
        owner_tile.T,
        stencil_cells.T,
        stencil_weights.T,
        inverse_error.T,
        profile_counts,
        correlation_inverse,
    )
    return control + untiled(returned, height, n_t)


def solution(mesh):
    tiles, levs = mesh.shape["tile"], mesh.shape["lev"]

    def step(*args):
        n_l, height, columns = args[0].shape
        dims = (tiles, levs, n_l, height, columns // 128, args[4].shape[0])
        return per_device(dims, *args)

    return jax.shard_map(
        step,
        mesh=mesh,
        in_specs=(P("lev", "tile", None), P("tile", None), P("tile", None), P("tile"), P("tile", None), P("tile", None),
                  P("tile", None), P("tile", "lev"), P()),
        out_specs=P("lev", "tile", None),
        check_vma=False,
    )
```

```python
import functools

import jax
import jax.numpy as jnp
from jax import lax
from jax.experimental import pallas as pl
from jax.experimental.pallas import tpu as pltpu
from jax.sharding import PartitionSpec as P

ITERS = 10
DEPTH = ITERS
NEAR = 5
SRC = 64
RANKS = 12
F32, BF16 = jnp.float32, jnp.bfloat16
NT = (((1,), (1,)), ((), ()))


def up_to(n, m):
    return -(-n // m) * m


def kernel(dims, ctrl, land, diff, owner, cells, weights, errors, counts, corr, out,
           u0, u1, u2, u3, hb, ca, cb, rh, sbuf, rbuf, wk, ln, er, acc, oh, vf, vt, sv, xt, adj, sb,
           halo_send, halo_recv, prof_send, prof_recv, lev_send, lev_recv):
    tiles, levs, n_l, height, n_t, stored = dims
    pitch, body, front = n_t + 1, up_to((n_t + 1) * n_l, 8), 8
    hw = up_to(n_t, 8)
    qn, qp = height * n_t, up_to(height * n_t, 128)
    slots = RANKS * SRC
    tile, lev = lax.axis_index("tile"), lax.axis_index("lev")
    lane = lax.broadcasted_iota(jnp.int32, (1, 128), 1)
    first, last = lane == 0, lane == 127

    barrier = pltpu.get_barrier_semaphore()

    def greet(i, carry):
        pl.semaphore_signal(barrier, inc=1, device_id={"tile": lax.rem(tile + i, tiles)})
        return carry

    lax.fori_loop(1, tiles, greet, 0)
    for i in range(1, levs):
        pl.semaphore_signal(barrier, inc=1, device_id={"lev": lax.rem(lev + i, levs)})

    rows_all = height + 2 * DEPTH

    def clear(r, carry):
        for u in (u0, u1, u2, u3):
            u[r, 0:front, :] = jnp.zeros((front, 128), F32)
            u[r, front + body:front + body + 8, :] = jnp.zeros((8, 128), F32)
        hb[r, 0:8, :] = jnp.zeros((8, 128), F32)
        hb[r, 8 + hw:16 + hw, :] = jnp.zeros((8, 128), F32)
        return carry

    lax.fori_loop(0, rows_all, clear, 0)

    def clear_halo(lo):
        def one(r, carry):
            for u in (u0, u3):
                u[r, front:front + body, :] = jnp.zeros((body, 128), F32)
            hb[r, 8:8 + hw, :] = jnp.zeros((hw, 128), F32)
            return carry

        lax.fori_loop(lo, lo + DEPTH, one, 0)

    @pl.when(tile == 0)
    def _():
        clear_halo(0)

    @pl.when(tile == tiles - 1)
    def _():
        clear_halo(DEPTH + height)

    for r in range(height):
        part, sub = r // 8, r % 8
        here = pl.ds(sub, n_t, stride=8)
        h = jnp.sqrt(land[part, here, :].astype(F32) * diff[part, here, :])
        hb[DEPTH + r, hw:8 + hw, :] = jnp.zeros((8, 128), F32)
        hb[DEPTH + r, 8:8 + n_t, :] = h
        rh[r, 0:n_t, :] = jnp.where(h > 0, 1.0 / h, 0.0)
        for l in range(n_l):
            at = front + pitch * l
            u0[DEPTH + r, at:at + n_t, :] = h * ctrl[l, part, here, :]
            for u in (u0, u3):
                end = at + pitch if l < n_l - 1 else front + body
                u[DEPTH + r, at + n_t:end, :] = jnp.zeros((end - at - n_t, 128), F32)

    spot = lax.broadcasted_iota(jnp.int32, (1, stored), 1)
    living = spot < counts[0]
    is_owner = jnp.where(
        (lax.broadcasted_iota(jnp.int32, (SRC, stored), 0) == owner[...]) & living, 1.0, 0.0
    )
    mine = is_owner.astype(BF16)
    before = jnp.where(
        lax.broadcasted_iota(jnp.int32, (stored, stored), 0)
        < lax.broadcasted_iota(jnp.int32, (stored, stored), 1), 1.0, 0.0
    ).astype(BF16)
    ahead = jnp.dot(mine, before, preferred_element_type=F32)
    rank = jnp.sum(ahead * is_owner, axis=0, keepdims=True)
    data = jnp.concatenate(
        [cells[...].astype(F32), weights[...], errors[...], jnp.zeros((8 - n_l, stored), F32)], axis=0
    )
    spread_out = jnp.concatenate([jnp.where(rank == float(r), data, 0.0) for r in range(16)], axis=0)
    message = jnp.zeros((SRC, 256), F32)
    left = spread_out
    for _ in range(3):
        piece = left.astype(BF16)
        message += lax.dot_general(mine, piece, NT, preferred_element_type=F32)
        left = left - piece.astype(F32)
    sbuf[...] = message.reshape(SRC, 1, 256)

    pl.semaphore_wait(barrier, tiles - 1 + levs - 1)

    def halo(which, side, chunk, root=False):
        lo, n = (0, NEAR) if chunk == 0 else (NEAR, DEPTH - NEAR)
        if side == 0:
            src, dst = DEPTH + lo, DEPTH + height + lo
        else:
            src, dst = height + DEPTH - lo - n, DEPTH - lo - n
        if root:
            a, b, which = hb.at[pl.ds(src, n), pl.ds(8, hw)], hb.at[pl.ds(dst, n), pl.ds(8, hw)], 2
        else:
            u = (u0, u3)[which]
            a, b = u.at[pl.ds(src, n), pl.ds(front, body)], u.at[pl.ds(dst, n), pl.ds(front, body)]
        return pltpu.make_async_remote_copy(
            src_ref=a, dst_ref=b, send_sem=halo_send.at[which, side, chunk], recv_sem=halo_recv.at[which, side, chunk],
            device_id={"tile": lax.rem(tile + (tiles - 1 if side == 0 else 1), tiles)},
        )

    def has(side):
        return tile > 0 if side == 0 else tile < tiles - 1

    def start_halo(which, chunk, root=False):
        for side in (0, 1):
            @pl.when(has(side))
            def _():
                halo(which, side, chunk, root).start()

    def wait_halo(which, chunk, root=False):
        for side in (0, 1):
            @pl.when(has(1 - side))
            def _():
                halo(which, side, chunk, root).wait_recv()

    def wait_sent(which, chunk, root=False):
        for side in (0, 1):
            @pl.when(has(side))
            def _():
                halo(which, side, chunk, root).wait_send()

    for chunk in (0, 1):
        start_halo(0, chunk, root=True)
        start_halo(0, chunk)

    def profile_copy(to, frm):
        return pltpu.make_async_remote_copy(
            src_ref=sbuf.at[to], dst_ref=rbuf.at[tile], send_sem=prof_send.at[to], recv_sem=prof_recv.at[frm],
            device_id={"tile": to},
        )

    def send_profiles(i, carry):
        to = lax.rem(tile + i, tiles)
        profile_copy(to, tile).start()
        return carry

    lax.fori_loop(1, tiles, send_profiles, 0)
    own = pltpu.make_async_copy(sbuf.at[tile], rbuf.at[tile], prof_recv.at[tile])
    own.start()

    def coefficients(lo, hi):
        def one(r, carry):
            h = hb[r, 8:8 + n_t, :]
            west = pltpu.roll(jnp.where(last, hb[r, 7:7 + n_t, :], h), 1, 1)
            east = pltpu.roll(jnp.where(first, hb[r, 9:9 + n_t, :], h), 127, 1)
            a = 1.0 - h * ((hb[r - 1, 8:8 + n_t, :] + hb[r + 1, 8:8 + n_t, :]) + (west + east))
            b = h * h
            for l in range(n_l):
                at = front + pitch * l
                end = at + pitch if l < n_l - 1 else front + body
                ca[r, at:at + n_t, :] = a
                cb[r, at:at + n_t, :] = b
                ca[r, at + n_t:end, :] = jnp.zeros((end - at - n_t, 128), F32)
                cb[r, at + n_t:end, :] = jnp.zeros((end - at - n_t, 128), F32)
            return carry

        lax.fori_loop(lo, hi, one, 0)

    mid = height // 2

    def sweep(src, dst, lo, n):
        def one(i, carry):
            for r in (DEPTH + lo + i, DEPTH + height - 1 - lo - i):
                made = []
                for j in range(front, front + body, 8):
                    here = pl.ds(j, 8)
                    c = src[r, here, :]
                    west = pltpu.roll(jnp.where(last, src[r, j - 1:j + 7, :], c), 1, 1)
                    east = pltpu.roll(jnp.where(first, src[r, j + 1:j + 9, :], c), 127, 1)
                    around = (src[r - 1, here, :] + src[r + 1, here, :]) + (west + east)
                    made.append(ca[r, here, :] * c + cb[r, here, :] * around)
                for j, value in zip(range(front, front + body, 8), made):
                    dst[r, pl.ds(j, 8), :] = value
            return carry

        lax.fori_loop(0, n, one, 0)

    def steps(begin, reach, total):
        sweep(begin, u1, *reach(1))

        def two(t, carry):
            sweep(u1, u2, *reach(2 * t))
            sweep(u2, u1, *reach(2 * t + 1))
            return carry

        lax.fori_loop(1, (total + 1) // 2, two, 0)
        if total % 2 == 0:
            sweep(u1, u2, *reach(total))

    def inner(begin):
        steps(begin, lambda s: (s, mid - s), mid - 1)

    def outer(begin, old, new):
        steps(begin, lambda s: (s - new, jnp.minimum(new - old, mid + new - s)), ITERS)

    coefficients(DEPTH + 1, DEPTH + height - 1)
    inner(u0)

    def got_profile(i, carry):
        frm = lax.rem(tile + i, tiles)
        profile_copy(frm, frm).wait_recv()
        return carry

    lax.fori_loop(1, tiles, got_profile, 0)
    own.wait()
    heard = jnp.concatenate([rbuf[...].reshape(SRC, 256), jnp.zeros((128 - SRC, 256), F32)], axis=0)
    turned = jnp.transpose(heard)
    for pair in range(RANKS // 2):
        both = turned[32 * pair:32 * pair + 16] + pltpu.roll(turned[32 * pair + 16:32 * pair + 32], SRC, 1)
        for k in range(4):
            where = pl.ds(k * slots + pair * 128, 128)
            cell = both[k:k + 1].astype(jnp.int32)
            wk[1:2, where] = (cell >> 7).astype(F32)
            ln[0:1, where] = cell & 127
            wk[0:1, where] = both[4 + k:5 + k]
        er[0:8, pl.ds(pair * 128, 128)] = both[8:16]

    def one_hots(i, carry):
        rows = lax.broadcasted_iota(jnp.int32, (128, 4 * slots), 0) + i * 128
        hot = jnp.where(rows == wk[1:2, :].astype(jnp.int32), 1.0, 0.0).astype(BF16)
        oh[pl.ds(pl.multiple_of(i * 128, 128), 128), :] = hot
        oh[pl.ds(pl.multiple_of(qp + i * 128, 128), 128), :] = hot
        return carry

    lax.fori_loop(0, qp // 128, one_hots, 0)

    wait_halo(0, 0, root=True)
    coefficients(DEPTH - NEAR + 1, DEPTH + 1)
    coefficients(DEPTH + height - 1, DEPTH + height + NEAR - 1)
    wait_halo(0, 0)
    outer(u0, 0, NEAR)
    wait_halo(0, 1, root=True)
    coefficients(1, DEPTH - NEAR + 1)
    coefficients(DEPTH + height + NEAR - 1, rows_all - 1)
    wait_halo(0, 1)
    for chunk in (0, 1):
        wait_sent(0, chunk, root=True)
        wait_sent(0, chunk)
    outer(u0, NEAR, DEPTH)

    for l in range(n_l):
        at = front + pitch * l
        for r in range(height):
            vf[l, r * n_t:(r + 1) * n_t, :] = rh[r, 0:n_t, :] * u2[DEPTH + r, at:at + n_t, :]
        if qp > qn:
            vf[l, qn:qp, :] = jnp.zeros((qp - qn, 128), F32)

    def turn(l, carry):
        here = pl.ds(pl.multiple_of(l * 128, 128), 128)
        value = jnp.transpose(vf[l, :, :])
        high = value.astype(BF16)
        vt[here, 0:qp] = high
        vt[here, qp:2 * qp] = (value - high.astype(F32)).astype(BF16)
        return carry

    lax.fori_loop(0, n_l, turn, 0)
    acc[...] = jnp.zeros_like(acc)
    split = slots // 256

    def pick(i, carry):
        where = pl.ds(pl.multiple_of(i * 256, 256), 256)
        into = pl.ds(pl.multiple_of(lax.rem(i, split) * 256, 256), 256)
        got = jnp.dot(vt[...], oh[:, where], preferred_element_type=F32)
        on = lax.broadcasted_iota(jnp.int32, (128, 256), 0) == ln[0:1, where]
        weight = wk[0:1, where]
        for l in range(n_l):
            value = jnp.where(on, got[l * 128:(l + 1) * 128], 0.0).reshape(16, 8, 256)
            acc[l, :, into] += jnp.sum(value, axis=0) * weight
        return carry

    lax.fori_loop(0, 4 * split, pick, 0)
    sb[lev, :, :] = jnp.zeros((8, slots), F32)
    for l in range(n_l):
        sb[lev, l:l + 1, :] = jnp.sum(acc[l], axis=0, keepdims=True) * er[l:l + 1, :]

    def level_copy(i, back=False):
        other = lax.rem(lev + (levs - i if back else i), levs)
        return pltpu.make_async_remote_copy(
            src_ref=sb.at[lev], dst_ref=sb.at[other if back else lev], send_sem=lev_send.at[other],
            recv_sem=lev_recv.at[other if back else lev], device_id={"lev": other},
        )

    for i in range(1, levs):
        level_copy(i).start()
    for i in range(1, levs):
        level_copy(i, back=True).wait_recv()
    coupled = [jnp.zeros((1, slots), F32) for _ in range(n_l)]
    for m in range(levs):
        for j in range(n_l):
            row = sb[m, j:j + 1, :]
            for l in range(n_l):
                coupled[l] = coupled[l] + corr[n_l * lev + l, n_l * m + j] * row
    for l in range(n_l):
        weighted = coupled[l] * er[l:l + 1, :]
        for k in range(4):
            where = pl.ds(k * slots, slots)
            value = weighted * wk[0:1, where]
            high = value.astype(BF16).astype(F32)
            sv[l, 0:1, where] = high
            sv[n_l + l, 0:1, where] = value - high

    def put(i, carry):
        rows = lax.broadcasted_iota(jnp.int32, (128, 4 * slots), 0)
        on = rows == ln[0:1, :]
        for g in range(2):
            xt[g * 128:(g + 1) * 128, :] = jnp.where(on, sv[2 * i + g, 0:1, :], 0.0).astype(BF16)
        adj[i, 0:qn, :] = lax.dot_general(oh[0:qn, :], xt[...], NT, preferred_element_type=F32)
        return carry

    lax.fori_loop(0, n_l, put, 0)
    for r in range(height):
        h = hb[DEPTH + r, 8:8 + n_t, :]
        for l in range(n_l):
            at = front + pitch * l
            low = n_l + l
            both = (
                adj[l // 2, r * n_t:(r + 1) * n_t, (l % 2) * 128:(l % 2 + 1) * 128]
                + adj[low // 2, r * n_t:(r + 1) * n_t, (low % 2) * 128:(low % 2 + 1) * 128]
            )
            u3[DEPTH + r, at:at + n_t, :] = h * both

    for chunk in (0, 1):
        start_halo(1, chunk)
    inner(u3)
    wait_halo(1, 0)
    outer(u3, 0, NEAR)
    wait_halo(1, 1)
    for chunk in (0, 1):
        wait_sent(1, chunk)
    outer(u3, NEAR, DEPTH)

    for r in range(height):
        part, here = r // 8, pl.ds(r % 8, n_t, stride=8)
        for l in range(n_l):
            at = front + pitch * l
            out[l, part, here, :] = rh[r, 0:n_t, :] * u2[DEPTH + r, at:at + n_t, :]

    def sent_profile(i, carry):
        profile_copy(lax.rem(tile + i, tiles), tile).wait_send()
        return carry

    lax.fori_loop(1, tiles, sent_profile, 0)
    for i in range(1, levs):
        level_copy(i).wait_send()


def tiled(x, height, n_t):
    lead = x.shape[:-2]
    n = len(lead)
    x = x.reshape(lead + (height // 8, 8, n_t, 128))
    x = jnp.swapaxes(x, n + 1, n + 2)
    return x.reshape(lead + (height // 8, n_t * 8, 128))


def untiled(x, height, n_t):
    lead = x.shape[:-3]
    n = len(lead)
    x = x.reshape(lead + (height // 8, n_t, 8, 128))
    x = jnp.swapaxes(x, n + 1, n + 2)
    return x.reshape(lead + (height, n_t * 128))


def per_device(dims, control, land_sea, diffusivity, profile_counts, owner_tile, stencil_cells, stencil_weights,
               inverse_error, correlation_inverse):
    tiles, levs, n_l, height, n_t, stored = dims
    body = up_to((n_t + 1) * n_l, 8)
    hw = up_to(n_t, 8)
    rows = height + 2 * DEPTH
    qn, qp = height * n_t, up_to(height * n_t, 128)
    slots = RANKS * SRC
    vmem = pl.BlockSpec(memory_space=pltpu.VMEM)
    smem = pl.BlockSpec(memory_space=pltpu.SMEM)
    returned = pl.pallas_call(
        functools.partial(kernel, dims),
        out_shape=jax.ShapeDtypeStruct((n_l, height // 8, n_t * 8, 128), F32),
        in_specs=[vmem] * 7 + [smem] * 2,
        out_specs=vmem,
        scratch_shapes=[
            *[pltpu.VMEM((rows, body + 16, 128), F32) for _ in range(4)],
            pltpu.VMEM((rows, hw + 16, 128), F32),
            pltpu.VMEM((rows, body + 16, 128), F32),
            pltpu.VMEM((rows, body + 16, 128), F32),
            pltpu.VMEM((height, hw, 128), F32),
            pltpu.VMEM((SRC, 1, 256), F32),
            pltpu.VMEM((SRC, 1, 256), F32),
            pltpu.VMEM((2, 4 * slots), F32),
            pltpu.VMEM((1, 4 * slots), jnp.int32),
            pltpu.VMEM((8, slots), F32),
            pltpu.VMEM((n_l, 8, slots), F32),
            pltpu.VMEM((2 * qp, 4 * slots), BF16),
            pltpu.VMEM((n_l, qp, 128), F32),
            pltpu.VMEM((n_l * 128, 2 * qp), BF16),
            pltpu.VMEM((2 * n_l, 1, 4 * slots), F32),
            pltpu.VMEM((256, 4 * slots), BF16),
            pltpu.VMEM((n_l, up_to(qn, 8), 256), F32),
            pltpu.VMEM((levs, 8, slots), F32),
            pltpu.SemaphoreType.DMA((3, 2, 2)),
            pltpu.SemaphoreType.DMA((3, 2, 2)),
            pltpu.SemaphoreType.DMA((SRC,)),
            pltpu.SemaphoreType.DMA((SRC,)),
            pltpu.SemaphoreType.DMA((levs,)),
            pltpu.SemaphoreType.DMA((levs,)),
        ],
        compiler_params=pltpu.CompilerParams(
            collective_id=0, has_side_effects=True, vmem_limit_bytes=60 * 2**20
        ),
    )(
        tiled(control, height, n_t),
        tiled(land_sea, height, n_t),
        tiled(diffusivity, height, n_t),
        owner_tile.T,
        stencil_cells.T,
        stencil_weights.T,
        inverse_error.T,
        profile_counts,
        correlation_inverse,
    )
    return control + untiled(returned, height, n_t)


def solution(mesh):
    tiles, levs = mesh.shape["tile"], mesh.shape["lev"]

    def step(*args):
        n_l, height, columns = args[0].shape
        dims = (tiles, levs, n_l, height, columns // 128, args[4].shape[0])
        return per_device(dims, *args)

    return jax.shard_map(
        step,
        mesh=mesh,
        in_specs=(P("lev", "tile", None), P("tile", None), P("tile", None), P("tile"), P("tile", None), P("tile", None),
                  P("tile", None), P("tile", "lev"), P()),
        out_specs=P("lev", "tile", None),
        check_vma=False,
    )
```

```python
import functools

import jax
import jax.numpy as jnp
from jax import lax
from jax.experimental import pallas as pl
from jax.experimental.pallas import tpu as pltpu
from jax.sharding import PartitionSpec as P

ITERS = 10
DEPTH = ITERS
CHUNK = 2
SRC = 64
RANKS = 12
F32, BF16 = jnp.float32, jnp.bfloat16
NT = (((1,), (1,)), ((), ()))


def up_to(n, m):
    return -(-n // m) * m


def kernel(dims, ctrl, land, diff, owner, cells, weights, errors, counts, corr, out,
           u0, u1, u2, u3, hb, ca, cb, rh, sbuf, rbuf, wk, ln, er, acc, oh, vf, vt, sv, xt, adj, sb,
           halo_send, halo_recv, prof_send, prof_recv, lev_send, lev_recv):
    tiles, levs, n_l, height, n_t, stored = dims
    pitch, body, front = n_t + 1, up_to((n_t + 1) * n_l, 8), 8
    hw = up_to(n_t, 8)
    qn, qp = height * n_t, up_to(height * n_t, 128)
    slots = RANKS * SRC
    tile, lev = lax.axis_index("tile"), lax.axis_index("lev")
    lane = lax.broadcasted_iota(jnp.int32, (1, 128), 1)
    first, last = lane == 0, lane == 127

    barrier = pltpu.get_barrier_semaphore()

    def greet(i, carry):
        pl.semaphore_signal(barrier, inc=1, device_id={"tile": lax.rem(tile + i, tiles)})
        return carry

    lax.fori_loop(1, tiles, greet, 0)
    for i in range(1, levs):
        pl.semaphore_signal(barrier, inc=1, device_id={"lev": lax.rem(lev + i, levs)})

    rows_all = height + 2 * DEPTH

    def clear(r, carry):
        for u in (u0, u1, u2, u3):
            u[r, 0:front, :] = jnp.zeros((front, 128), F32)
            u[r, front + body:front + body + 8, :] = jnp.zeros((8, 128), F32)
        hb[r, 0:8, :] = jnp.zeros((8, 128), F32)
        hb[r, 8 + hw:16 + hw, :] = jnp.zeros((8, 128), F32)
        return carry

    lax.fori_loop(0, rows_all, clear, 0)

    def clear_halo(lo):
        def one(r, carry):
            for u in (u0, u3):
                u[r, front:front + body, :] = jnp.zeros((body, 128), F32)
            hb[r, 8:8 + hw, :] = jnp.zeros((hw, 128), F32)
            return carry

        lax.fori_loop(lo, lo + DEPTH, one, 0)

    @pl.when(tile == 0)
    def _():
        clear_halo(0)

    @pl.when(tile == tiles - 1)
    def _():
        clear_halo(DEPTH + height)

    for r in range(height):
        part, sub = r // 8, r % 8
        here = pl.ds(sub, n_t, stride=8)
        h = jnp.sqrt(land[part, here, :].astype(F32) * diff[part, here, :])
        hb[DEPTH + r, hw:8 + hw, :] = jnp.zeros((8, 128), F32)
        hb[DEPTH + r, 8:8 + n_t, :] = h
        rh[r, 0:n_t, :] = jnp.where(h > 0, 1.0 / h, 0.0)
        for l in range(n_l):
            at = front + pitch * l
            u0[DEPTH + r, at:at + n_t, :] = h * ctrl[l, part, here, :]
            for u in (u0, u3):
                end = at + pitch if l < n_l - 1 else front + body
                u[DEPTH + r, at + n_t:end, :] = jnp.zeros((end - at - n_t, 128), F32)

    pl.semaphore_wait(barrier, tiles - 1 + levs - 1)

    def halo(which, side, chunk, root=False):
        lo, n = chunk * CHUNK, CHUNK
        if side == 0:
            src, dst = DEPTH + lo, DEPTH + height + lo
        else:
            src, dst = height + DEPTH - lo - n, DEPTH - lo - n
        if root:
            a, b, which = hb.at[pl.ds(src, n), pl.ds(8, hw)], hb.at[pl.ds(dst, n), pl.ds(8, hw)], 2
        else:
            u = (u0, u3)[which]
            a, b = u.at[pl.ds(src, n), pl.ds(front, body)], u.at[pl.ds(dst, n), pl.ds(front, body)]
        return pltpu.make_async_remote_copy(
            src_ref=a, dst_ref=b, send_sem=halo_send.at[which, side, chunk], recv_sem=halo_recv.at[which, side, chunk],
            device_id={"tile": lax.rem(tile + (tiles - 1 if side == 0 else 1), tiles)},
        )

    def has(side):
        return tile > 0 if side == 0 else tile < tiles - 1

    def start_halo(which, chunk, root=False):
        for side in (0, 1):
            @pl.when(has(side))
            def _():
                halo(which, side, chunk, root).start()

    def wait_halo(which, chunk, root=False):
        for side in (0, 1):
            @pl.when(has(1 - side))
            def _():
                halo(which, side, chunk, root).wait_recv()

    def wait_sent(which, chunk, root=False):
        for side in (0, 1):
            @pl.when(has(side))
            def _():
                halo(which, side, chunk, root).wait_send()

    chunks = DEPTH // CHUNK

    def start_first(chunk, carry):
        start_halo(0, chunk, root=True)
        start_halo(0, chunk)
        return carry

    lax.fori_loop(0, chunks, start_first, 0)


    spot = lax.broadcasted_iota(jnp.int32, (1, stored), 1)
    living = spot < counts[0]
    is_owner = jnp.where(
        (lax.broadcasted_iota(jnp.int32, (SRC, stored), 0) == owner[...]) & living, 1.0, 0.0
    )
    mine = is_owner.astype(BF16)
    before = jnp.where(
        lax.broadcasted_iota(jnp.int32, (stored, stored), 0)
        < lax.broadcasted_iota(jnp.int32, (stored, stored), 1), 1.0, 0.0
    ).astype(BF16)
    ahead = jnp.dot(mine, before, preferred_element_type=F32)
    rank = jnp.sum(ahead * is_owner, axis=0, keepdims=True)
    data = jnp.concatenate(
        [cells[...].astype(F32), weights[...], errors[...], jnp.zeros((8 - n_l, stored), F32)], axis=0
    )
    spread_out = jnp.concatenate([jnp.where(rank == float(r), data, 0.0) for r in range(16)], axis=0)
    message = jnp.zeros((SRC, 256), F32)
    left = spread_out
    for _ in range(3):
        piece = left.astype(BF16)
        message += lax.dot_general(mine, piece, NT, preferred_element_type=F32)
        left = left - piece.astype(F32)
    sbuf[...] = message.reshape(SRC, 1, 256)

    def profile_copy(to, frm):
        return pltpu.make_async_remote_copy(
            src_ref=sbuf.at[to], dst_ref=rbuf.at[tile], send_sem=prof_send.at[to], recv_sem=prof_recv.at[frm],
            device_id={"tile": to},
        )

    def send_profiles(i, carry):
        to = lax.rem(tile + i, tiles)
        profile_copy(to, tile).start()
        return carry

    lax.fori_loop(1, tiles, send_profiles, 0)
    own = pltpu.make_async_copy(sbuf.at[tile], rbuf.at[tile], prof_recv.at[tile])
    own.start()

    def coefficients(lo, hi):
        def one(r, carry):
            h = hb[r, 8:8 + n_t, :]
            west = pltpu.roll(jnp.where(last, hb[r, 7:7 + n_t, :], h), 1, 1)
            east = pltpu.roll(jnp.where(first, hb[r, 9:9 + n_t, :], h), 127, 1)
            a = 1.0 - h * ((hb[r - 1, 8:8 + n_t, :] + hb[r + 1, 8:8 + n_t, :]) + (west + east))
            b = h * h
            for l in range(n_l):
                at = front + pitch * l
                end = at + pitch if l < n_l - 1 else front + body
                ca[r, at:at + n_t, :] = a
                cb[r, at:at + n_t, :] = b
                ca[r, at + n_t:end, :] = jnp.zeros((end - at - n_t, 128), F32)
                cb[r, at + n_t:end, :] = jnp.zeros((end - at - n_t, 128), F32)
            return carry

        lax.fori_loop(lo, hi, one, 0)

    mid = height // 2

    def sweep(src, dst, lo, n):
        def one(i, carry):
            for r in (DEPTH + lo + i, DEPTH + height - 1 - lo - i):
                made = []
                for j in range(front, front + body, 8):
                    here = pl.ds(j, 8)
                    c = src[r, here, :]
                    west = pltpu.roll(jnp.where(last, src[r, j - 1:j + 7, :], c), 1, 1)
                    east = pltpu.roll(jnp.where(first, src[r, j + 1:j + 9, :], c), 127, 1)
                    around = (src[r - 1, here, :] + src[r + 1, here, :]) + (west + east)
                    made.append(ca[r, here, :] * c + cb[r, here, :] * around)
                for j, value in zip(range(front, front + body, 8), made):
                    dst[r, pl.ds(j, 8), :] = value
            return carry

        lax.fori_loop(0, n, one, 0)

    def steps(begin, reach, total):
        sweep(begin, u1, *reach(1))

        def two(t, carry):
            sweep(u1, u2, *reach(2 * t))
            sweep(u2, u1, *reach(2 * t + 1))
            return carry

        lax.fori_loop(1, (total + 1) // 2, two, 0)
        if total % 2 == 0:
            sweep(u1, u2, *reach(total))

    def inner(begin):
        steps(begin, lambda s: (s, mid - s), mid - 1)

    def nearest(begin):
        steps(begin, lambda s: (s - CHUNK, jnp.minimum(CHUNK, mid + CHUNK - s)), ITERS)

    def both_ends(src, dst, lo):
        for top in (DEPTH + lo, DEPTH + height - lo - CHUNK):
            for half in range(front, front + body, body // 2):
                made = []
                for j in range(half, half + body // 2, 8):
                    here = pl.ds(j, 8)
                    c = [src[top + i, here, :] for i in range(-1, CHUNK + 1)]
                    for i in range(CHUNK):
                        r, own = top + i, c[i + 1]
                        west = pltpu.roll(jnp.where(last, src[r, j - 1:j + 7, :], own), 1, 1)
                        east = pltpu.roll(jnp.where(first, src[r, j + 1:j + 9, :], own), 127, 1)
                        around = (c[i] + c[i + 2]) + (west + east)
                        made.append((r, here, ca[r, here, :] * own + cb[r, here, :] * around))
                for r, here, value in made:
                    dst[r, here, :] = value

    def farther(begin, chunk):
        lo = -CHUNK * (chunk + 1)
        both_ends(begin, u1, lo + 1)

        def two(t, carry):
            both_ends(u1, u2, lo + 2 * t)
            both_ends(u2, u1, lo + 2 * t + 1)
            return carry

        lax.fori_loop(1, ITERS // 2, two, 0)
        both_ends(u1, u2, lo + ITERS)

    coefficients(DEPTH + 1, DEPTH + height - 1)
    inner(u0)

    def got_profile(i, carry):
        frm = lax.rem(tile + i, tiles)
        profile_copy(frm, frm).wait_recv()
        return carry

    lax.fori_loop(1, tiles, got_profile, 0)
    own.wait()
    heard = jnp.concatenate([rbuf[...].reshape(SRC, 256), jnp.zeros((128 - SRC, 256), F32)], axis=0)
    turned = jnp.transpose(heard)
    for pair in range(RANKS // 2):
        both = turned[32 * pair:32 * pair + 16] + pltpu.roll(turned[32 * pair + 16:32 * pair + 32], SRC, 1)
        for k in range(4):
            where = pl.ds(k * slots + pair * 128, 128)
            cell = both[k:k + 1].astype(jnp.int32)
            wk[1:2, where] = (cell >> 7).astype(F32)
            ln[0:1, where] = cell & 127
            wk[0:1, where] = both[4 + k:5 + k]
        er[0:8, pl.ds(pair * 128, 128)] = both[8:16]

    def one_hots(i, carry):
        rows = lax.broadcasted_iota(jnp.int32, (128, 4 * slots), 0) + i * 128
        hot = jnp.where(rows == wk[1:2, :].astype(jnp.int32), 1.0, 0.0).astype(BF16)
        oh[pl.ds(pl.multiple_of(i * 128, 128), 128), :] = hot
        oh[pl.ds(pl.multiple_of(qp + i * 128, 128), 128), :] = hot
        return carry

    lax.fori_loop(0, qp // 128, one_hots, 0)

    def more_roots(chunk):
        wait_halo(0, chunk, root=True)
        coefficients(DEPTH - CHUNK * chunk - 1, DEPTH - CHUNK * chunk + 1)
        coefficients(DEPTH + height + CHUNK * chunk - 1, DEPTH + height + CHUNK * chunk + 1)
        wait_halo(0, chunk)

    more_roots(0)
    nearest(u0)

    def arrived(chunk, carry):
        more_roots(chunk)
        farther(u0, chunk)
        return carry

    lax.fori_loop(1, chunks, arrived, 0)

    def all_sent(chunk, carry):
        wait_sent(0, chunk, root=True)
        wait_sent(0, chunk)
        return carry

    lax.fori_loop(0, chunks, all_sent, 0)

    for l in range(n_l):
        at = front + pitch * l
        for r in range(height):
            vf[l, r * n_t:(r + 1) * n_t, :] = rh[r, 0:n_t, :] * u2[DEPTH + r, at:at + n_t, :]
        if qp > qn:
            vf[l, qn:qp, :] = jnp.zeros((qp - qn, 128), F32)

    def turn(l, carry):
        here = pl.ds(pl.multiple_of(l * 128, 128), 128)
        value = jnp.transpose(vf[l, :, :])
        high = value.astype(BF16)
        vt[here, 0:qp] = high
        vt[here, qp:2 * qp] = (value - high.astype(F32)).astype(BF16)
        return carry

    lax.fori_loop(0, n_l, turn, 0)
    acc[...] = jnp.zeros_like(acc)
    split = slots // 256

    def pick(i, carry):
        where = pl.ds(pl.multiple_of(i * 256, 256), 256)
        into = pl.ds(pl.multiple_of(lax.rem(i, split) * 256, 256), 256)
        got = jnp.dot(vt[...], oh[:, where], preferred_element_type=F32)
        on = lax.broadcasted_iota(jnp.int32, (128, 256), 0) == ln[0:1, where]
        weight = wk[0:1, where]
        for l in range(n_l):
            value = jnp.where(on, got[l * 128:(l + 1) * 128], 0.0).reshape(16, 8, 256)
            acc[l, :, into] += jnp.sum(value, axis=0) * weight
        return carry

    lax.fori_loop(0, 4 * split, pick, 0)
    sb[lev, :, :] = jnp.zeros((8, slots), F32)
    for l in range(n_l):
        sb[lev, l:l + 1, :] = jnp.sum(acc[l], axis=0, keepdims=True) * er[l:l + 1, :]

    def level_copy(i, back=False):
        other = lax.rem(lev + (levs - i if back else i), levs)
        return pltpu.make_async_remote_copy(
            src_ref=sb.at[lev], dst_ref=sb.at[other if back else lev], send_sem=lev_send.at[other],
            recv_sem=lev_recv.at[other if back else lev], device_id={"lev": other},
        )

    for i in range(1, levs):
        level_copy(i).start()
    for i in range(1, levs):
        level_copy(i, back=True).wait_recv()
    coupled = [jnp.zeros((1, slots), F32) for _ in range(n_l)]
    for m in range(levs):
        for j in range(n_l):
            row = sb[m, j:j + 1, :]
            for l in range(n_l):
                coupled[l] = coupled[l] + corr[n_l * lev + l, n_l * m + j] * row
    for l in range(n_l):
        weighted = coupled[l] * er[l:l + 1, :]
        for k in range(4):
            where = pl.ds(k * slots, slots)
            value = weighted * wk[0:1, where]
            high = value.astype(BF16).astype(F32)
            sv[l, 0:1, where] = high
            sv[n_l + l, 0:1, where] = value - high

    def put(i, carry):
        rows = lax.broadcasted_iota(jnp.int32, (128, 4 * slots), 0)
        on = rows == ln[0:1, :]
        for g in range(2):
            xt[g * 128:(g + 1) * 128, :] = jnp.where(on, sv[2 * i + g, 0:1, :], 0.0).astype(BF16)
        adj[i, 0:qn, :] = lax.dot_general(oh[0:qn, :], xt[...], NT, preferred_element_type=F32)
        return carry

    lax.fori_loop(0, n_l, put, 0)
    for r in range(height):
        h = hb[DEPTH + r, 8:8 + n_t, :]
        for l in range(n_l):
            at = front + pitch * l
            low = n_l + l
            both = (
                adj[l // 2, r * n_t:(r + 1) * n_t, (l % 2) * 128:(l % 2 + 1) * 128]
                + adj[low // 2, r * n_t:(r + 1) * n_t, (low % 2) * 128:(low % 2 + 1) * 128]
            )
            u3[DEPTH + r, at:at + n_t, :] = h * both

    def start_second(chunk, carry):
        start_halo(1, chunk)
        return carry

    lax.fori_loop(0, chunks, start_second, 0)
    inner(u3)
    wait_halo(1, 0)
    nearest(u3)

    def arrived_again(chunk, carry):
        wait_halo(1, chunk)
        farther(u3, chunk)
        return carry

    lax.fori_loop(1, chunks, arrived_again, 0)

    def all_sent_again(chunk, carry):
        wait_sent(1, chunk)
        return carry

    lax.fori_loop(0, chunks, all_sent_again, 0)

    for r in range(height):
        part, here = r // 8, pl.ds(r % 8, n_t, stride=8)
        for l in range(n_l):
            at = front + pitch * l
            out[l, part, here, :] = rh[r, 0:n_t, :] * u2[DEPTH + r, at:at + n_t, :]

    def sent_profile(i, carry):
        profile_copy(lax.rem(tile + i, tiles), tile).wait_send()
        return carry

    lax.fori_loop(1, tiles, sent_profile, 0)
    for i in range(1, levs):
        level_copy(i).wait_send()


def tiled(x, height, n_t):
    lead = x.shape[:-2]
    n = len(lead)
    x = x.reshape(lead + (height // 8, 8, n_t, 128))
    x = jnp.swapaxes(x, n + 1, n + 2)
    return x.reshape(lead + (height // 8, n_t * 8, 128))


def untiled(x, height, n_t):
    lead = x.shape[:-3]
    n = len(lead)
    x = x.reshape(lead + (height // 8, n_t, 8, 128))
    x = jnp.swapaxes(x, n + 1, n + 2)
    return x.reshape(lead + (height, n_t * 128))


def per_device(dims, control, land_sea, diffusivity, profile_counts, owner_tile, stencil_cells, stencil_weights,
               inverse_error, correlation_inverse):
    tiles, levs, n_l, height, n_t, stored = dims
    body = up_to((n_t + 1) * n_l, 8)
    hw = up_to(n_t, 8)
    rows = height + 2 * DEPTH
    qn, qp = height * n_t, up_to(height * n_t, 128)
    slots = RANKS * SRC
    vmem = pl.BlockSpec(memory_space=pltpu.VMEM)
    smem = pl.BlockSpec(memory_space=pltpu.SMEM)
    returned = pl.pallas_call(
        functools.partial(kernel, dims),
        out_shape=jax.ShapeDtypeStruct((n_l, height // 8, n_t * 8, 128), F32),
        in_specs=[vmem] * 7 + [smem] * 2,
        out_specs=vmem,
        scratch_shapes=[
            *[pltpu.VMEM((rows, body + 16, 128), F32) for _ in range(4)],
            pltpu.VMEM((rows, hw + 16, 128), F32),
            pltpu.VMEM((rows, body + 16, 128), F32),
            pltpu.VMEM((rows, body + 16, 128), F32),
            pltpu.VMEM((height, hw, 128), F32),
            pltpu.VMEM((SRC, 1, 256), F32),
            pltpu.VMEM((SRC, 1, 256), F32),
            pltpu.VMEM((2, 4 * slots), F32),
            pltpu.VMEM((1, 4 * slots), jnp.int32),
            pltpu.VMEM((8, slots), F32),
            pltpu.VMEM((n_l, 8, slots), F32),
            pltpu.VMEM((2 * qp, 4 * slots), BF16),
            pltpu.VMEM((n_l, qp, 128), F32),
            pltpu.VMEM((n_l * 128, 2 * qp), BF16),
            pltpu.VMEM((2 * n_l, 1, 4 * slots), F32),
            pltpu.VMEM((256, 4 * slots), BF16),
            pltpu.VMEM((n_l, up_to(qn, 8), 256), F32),
            pltpu.VMEM((levs, 8, slots), F32),
            pltpu.SemaphoreType.DMA((3, 2, DEPTH // CHUNK)),
            pltpu.SemaphoreType.DMA((3, 2, DEPTH // CHUNK)),
            pltpu.SemaphoreType.DMA((SRC,)),
            pltpu.SemaphoreType.DMA((SRC,)),
            pltpu.SemaphoreType.DMA((levs,)),
            pltpu.SemaphoreType.DMA((levs,)),
        ],
        compiler_params=pltpu.CompilerParams(
            collective_id=0, has_side_effects=True, vmem_limit_bytes=60 * 2**20
        ),
    )(
        tiled(control, height, n_t),
        tiled(land_sea, height, n_t),
        tiled(diffusivity, height, n_t),
        owner_tile.T,
        stencil_cells.T,
        stencil_weights.T,
        inverse_error.T,
        profile_counts,
        correlation_inverse,
    )
    return control + untiled(returned, height, n_t)


def solution(mesh):
    tiles, levs = mesh.shape["tile"], mesh.shape["lev"]

    def step(*args):
        n_l, height, columns = args[0].shape
        dims = (tiles, levs, n_l, height, columns // 128, args[4].shape[0])
        return per_device(dims, *args)

    return jax.shard_map(
        step,
        mesh=mesh,
        in_specs=(P("lev", "tile", None), P("tile", None), P("tile", None), P("tile"), P("tile", None), P("tile", None),
                  P("tile", None), P("tile", "lev"), P()),
        out_specs=P("lev", "tile", None),
        check_vma=False,
    )
```

```python
import functools

import jax
import jax.numpy as jnp
from jax import lax
from jax.experimental import pallas as pl
from jax.experimental.pallas import tpu as pltpu
from jax.sharding import PartitionSpec as P

ITERS = 10
DEPTH = ITERS
CHUNK = 2
SRC = 64
RANKS = 12
F32, BF16 = jnp.float32, jnp.bfloat16
NT = (((1,), (1,)), ((), ()))


def up_to(n, m):
    return -(-n // m) * m


def kernel(dims, ctrl, land, diff, owner, cells, weights, errors, counts, corr, out,
           u0, u1, u2, u3, hb, ca, cb, rh, sbuf, rbuf, wk, ln, er, acc, oh, vf, vt, sv, xt, adj, sb,
           halo_send, halo_recv, prof_send, prof_recv, lev_send, lev_recv):
    tiles, levs, n_l, height, n_t, stored = dims
    pitch, body, front = n_t + 1, up_to((n_t + 1) * n_l, 8), 8
    hw = up_to(n_t, 8)
    qn, qp = height * n_t, up_to(height * n_t, 128)
    slots = RANKS * SRC
    tile, lev = lax.axis_index("tile"), lax.axis_index("lev")
    lane = lax.broadcasted_iota(jnp.int32, (1, 128), 1)
    first, last = lane == 0, lane == 127

    barrier = pltpu.get_barrier_semaphore()

    def each_other(act):
        group = next(g for g in (7, 5, 3, 1) if (tiles - 1) % g == 0)

        def some(i, carry):
            for k in range(1, group + 1):
                act(lax.rem(tile + i * group + k, tiles))
            return carry

        lax.fori_loop(0, (tiles - 1) // group, some, 0)

    each_other(lambda t: pl.semaphore_signal(barrier, inc=1, device_id={"tile": t}))
    for i in range(1, levs):
        pl.semaphore_signal(barrier, inc=1, device_id={"lev": lax.rem(lev + i, levs)})

    rows_all = height + 2 * DEPTH

    def clear(r, carry):
        for u in (u0, u1, u2, u3):
            u[r, 0:front, :] = jnp.zeros((front, 128), F32)
            u[r, front + body:front + body + 8, :] = jnp.zeros((8, 128), F32)
        hb[r, 0:8, :] = jnp.zeros((8, 128), F32)
        hb[r, 8 + hw:16 + hw, :] = jnp.zeros((8, 128), F32)
        return carry

    lax.fori_loop(0, rows_all, clear, 0)

    def clear_halo(lo):
        def one(r, carry):
            for u in (u0, u3):
                u[r, front:front + body, :] = jnp.zeros((body, 128), F32)
            hb[r, 8:8 + hw, :] = jnp.zeros((hw, 128), F32)
            return carry

        lax.fori_loop(lo, lo + DEPTH, one, 0)

    @pl.when(tile == 0)
    def _():
        clear_halo(0)

    @pl.when(tile == tiles - 1)
    def _():
        clear_halo(DEPTH + height)

    for r in range(height):
        part, sub = r // 8, r % 8
        here = pl.ds(sub, n_t, stride=8)
        h = jnp.sqrt(land[part, here, :].astype(F32) * diff[part, here, :])
        hb[DEPTH + r, hw:8 + hw, :] = jnp.zeros((8, 128), F32)
        hb[DEPTH + r, 8:8 + n_t, :] = h
        rh[r, 0:n_t, :] = jnp.where(h > 0, 1.0 / h, 0.0)
        for l in range(n_l):
            at = front + pitch * l
            u0[DEPTH + r, at:at + n_t, :] = h * ctrl[l, part, here, :]
            for u in (u0, u3):
                end = at + pitch if l < n_l - 1 else front + body
                u[DEPTH + r, at + n_t:end, :] = jnp.zeros((end - at - n_t, 128), F32)

    pl.semaphore_wait(barrier, tiles - 1 + levs - 1)

    def halo(which, side, chunk, root=False):
        lo, n = chunk * CHUNK, CHUNK
        if side == 0:
            src, dst = DEPTH + lo, DEPTH + height + lo
        else:
            src, dst = height + DEPTH - lo - n, DEPTH - lo - n
        if root:
            a, b, which = hb.at[pl.ds(src, n), pl.ds(8, hw)], hb.at[pl.ds(dst, n), pl.ds(8, hw)], 2
        else:
            u = (u0, u3)[which]
            a, b = u.at[pl.ds(src, n), pl.ds(front, body)], u.at[pl.ds(dst, n), pl.ds(front, body)]
        return pltpu.make_async_remote_copy(
            src_ref=a, dst_ref=b, send_sem=halo_send.at[which, side, chunk], recv_sem=halo_recv.at[which, side, chunk],
            device_id={"tile": lax.rem(tile + (tiles - 1 if side == 0 else 1), tiles)},
        )

    def has(side):
        return tile > 0 if side == 0 else tile < tiles - 1

    def start_halo(which, chunk, root=False):
        for side in (0, 1):
            @pl.when(has(side))
            def _():
                halo(which, side, chunk, root).start()

    def wait_halo(which, chunk, root=False):
        for side in (0, 1):
            @pl.when(has(1 - side))
            def _():
                halo(which, side, chunk, root).wait_recv()

    def wait_sent(which, chunk, root=False):
        for side in (0, 1):
            @pl.when(has(side))
            def _():
                halo(which, side, chunk, root).wait_send()

    chunks = DEPTH // CHUNK

    def start_first(chunk, carry):
        start_halo(0, chunk, root=True)
        start_halo(0, chunk)
        return carry

    lax.fori_loop(0, chunks, start_first, 0)


    spot = lax.broadcasted_iota(jnp.int32, (1, stored), 1)
    living = spot < counts[0]
    is_owner = jnp.where(
        (lax.broadcasted_iota(jnp.int32, (SRC, stored), 0) == owner[...]) & living, 1.0, 0.0
    )
    mine = is_owner.astype(BF16)
    before = jnp.where(
        lax.broadcasted_iota(jnp.int32, (stored, stored), 0)
        < lax.broadcasted_iota(jnp.int32, (stored, stored), 1), 1.0, 0.0
    ).astype(BF16)
    ahead = jnp.dot(mine, before, preferred_element_type=F32)
    rank = jnp.sum(ahead * is_owner, axis=0, keepdims=True)
    data = jnp.concatenate(
        [cells[...].astype(F32), weights[...], errors[...], jnp.zeros((8 - n_l, stored), F32)], axis=0
    )
    spread_out = jnp.concatenate([jnp.where(rank == float(r), data, 0.0) for r in range(16)], axis=0)
    message = jnp.zeros((SRC, 256), F32)
    left = spread_out
    for _ in range(3):
        piece = left.astype(BF16)
        message += lax.dot_general(mine, piece, NT, preferred_element_type=F32)
        left = left - piece.astype(F32)
    sbuf[...] = message.reshape(SRC, 1, 256)

    def profile_copy(src, dst, to):
        return pltpu.make_async_remote_copy(
            src_ref=src, dst_ref=dst, send_sem=prof_send.at[0], recv_sem=prof_recv.at[0], device_id={"tile": to}
        )

    each_other(lambda t: profile_copy(sbuf.at[t], rbuf.at[tile], t).start())
    own = pltpu.make_async_copy(sbuf.at[tile], rbuf.at[tile], prof_recv.at[1])
    own.start()
    others = pl.ds(0, tiles - 1)
    every = profile_copy(sbuf.at[others], rbuf.at[others], lax.rem(tile + 1, tiles))

    def coefficients(lo, hi):
        def one(r, carry):
            h = hb[r, 8:8 + n_t, :]
            west = pltpu.roll(jnp.where(last, hb[r, 7:7 + n_t, :], h), 1, 1)
            east = pltpu.roll(jnp.where(first, hb[r, 9:9 + n_t, :], h), 127, 1)
            a = 1.0 - h * ((hb[r - 1, 8:8 + n_t, :] + hb[r + 1, 8:8 + n_t, :]) + (west + east))
            b = h * h
            for l in range(n_l):
                at = front + pitch * l
                end = at + pitch if l < n_l - 1 else front + body
                ca[r, at:at + n_t, :] = a
                cb[r, at:at + n_t, :] = b
                ca[r, at + n_t:end, :] = jnp.zeros((end - at - n_t, 128), F32)
                cb[r, at + n_t:end, :] = jnp.zeros((end - at - n_t, 128), F32)
            return carry

        lax.fori_loop(lo, hi, one, 0)

    mid = height // 2

    def sweep(src, dst, lo, n):
        def one(i, carry):
            for r in (DEPTH + lo + i, DEPTH + height - 1 - lo - i):
                made = []
                for j in range(front, front + body, 8):
                    here = pl.ds(j, 8)
                    c = src[r, here, :]
                    west = pltpu.roll(jnp.where(last, src[r, j - 1:j + 7, :], c), 1, 1)
                    east = pltpu.roll(jnp.where(first, src[r, j + 1:j + 9, :], c), 127, 1)
                    around = (src[r - 1, here, :] + src[r + 1, here, :]) + (west + east)
                    made.append(ca[r, here, :] * c + cb[r, here, :] * around)
                for j, value in zip(range(front, front + body, 8), made):
                    dst[r, pl.ds(j, 8), :] = value
            return carry

        lax.fori_loop(0, n, one, 0)

    def steps(begin, reach, total):
        sweep(begin, u1, *reach(1))

        def two(t, carry):
            sweep(u1, u2, *reach(2 * t))
            sweep(u2, u1, *reach(2 * t + 1))
            return carry

        lax.fori_loop(1, (total + 1) // 2, two, 0)
        if total % 2 == 0:
            sweep(u1, u2, *reach(total))

    def inner(begin):
        steps(begin, lambda s: (s, mid - s), mid - 1)

    def nearest(begin):
        steps(begin, lambda s: (s - CHUNK, jnp.minimum(CHUNK, mid + CHUNK - s)), ITERS)

    def both_ends(src, dst, lo):
        for top in (DEPTH + lo, DEPTH + height - lo - CHUNK):
            for half in range(front, front + body, body // 2):
                made = []
                for j in range(half, half + body // 2, 8):
                    here = pl.ds(j, 8)
                    c = [src[top + i, here, :] for i in range(-1, CHUNK + 1)]
                    for i in range(CHUNK):
                        r, own = top + i, c[i + 1]
                        west = pltpu.roll(jnp.where(last, src[r, j - 1:j + 7, :], own), 1, 1)
                        east = pltpu.roll(jnp.where(first, src[r, j + 1:j + 9, :], own), 127, 1)
                        around = (c[i] + c[i + 2]) + (west + east)
                        made.append((r, here, ca[r, here, :] * own + cb[r, here, :] * around))
                for r, here, value in made:
                    dst[r, here, :] = value

    def farther(begin, chunk):
        lo = -CHUNK * (chunk + 1)
        both_ends(begin, u1, lo + 1)

        def two(t, carry):
            both_ends(u1, u2, lo + 2 * t)
            both_ends(u2, u1, lo + 2 * t + 1)
            return carry

        lax.fori_loop(1, ITERS // 2, two, 0)
        both_ends(u1, u2, lo + ITERS)

    coefficients(DEPTH + 1, DEPTH + height - 1)
    inner(u0)

    every.wait_recv()
    own.wait()
    heard = jnp.concatenate([rbuf[...].reshape(SRC, 256), jnp.zeros((128 - SRC, 256), F32)], axis=0)
    turned = jnp.transpose(heard)
    for pair in range(RANKS // 2):
        both = turned[32 * pair:32 * pair + 16] + pltpu.roll(turned[32 * pair + 16:32 * pair + 32], SRC, 1)
        for k in range(4):
            where = pl.ds(k * slots + pair * 128, 128)
            cell = both[k:k + 1].astype(jnp.int32)
            wk[1:2, where] = (cell >> 7).astype(F32)
            ln[0:1, where] = cell & 127
            wk[0:1, where] = both[4 + k:5 + k]
        er[0:8, pl.ds(pair * 128, 128)] = both[8:16]

    def one_hots(i, carry):
        rows = lax.broadcasted_iota(jnp.int32, (128, 4 * slots), 0) + i * 128
        hot = jnp.where(rows == wk[1:2, :].astype(jnp.int32), 1.0, 0.0).astype(BF16)
        oh[pl.ds(pl.multiple_of(i * 128, 128), 128), :] = hot
        oh[pl.ds(pl.multiple_of(qp + i * 128, 128), 128), :] = hot
        return carry

    lax.fori_loop(0, qp // 128, one_hots, 0)

    def more_roots(chunk):
        wait_halo(0, chunk, root=True)
        coefficients(DEPTH - CHUNK * chunk - 1, DEPTH - CHUNK * chunk + 1)
        coefficients(DEPTH + height + CHUNK * chunk - 1, DEPTH + height + CHUNK * chunk + 1)
        wait_halo(0, chunk)

    more_roots(0)
    nearest(u0)

    def arrived(chunk, carry):
        more_roots(chunk)
        farther(u0, chunk)
        return carry

    lax.fori_loop(1, chunks, arrived, 0)

    def all_sent(chunk, carry):
        wait_sent(0, chunk, root=True)
        wait_sent(0, chunk)
        return carry

    lax.fori_loop(0, chunks, all_sent, 0)

    for l in range(n_l):
        at = front + pitch * l
        for r in range(height):
            vf[l, r * n_t:(r + 1) * n_t, :] = rh[r, 0:n_t, :] * u2[DEPTH + r, at:at + n_t, :]
        if qp > qn:
            vf[l, qn:qp, :] = jnp.zeros((qp - qn, 128), F32)

    def turn(l, carry):
        here = pl.ds(pl.multiple_of(l * 128, 128), 128)
        value = jnp.transpose(vf[l, :, :])
        high = value.astype(BF16)
        vt[here, 0:qp] = high
        vt[here, qp:2 * qp] = (value - high.astype(F32)).astype(BF16)
        return carry

    lax.fori_loop(0, n_l, turn, 0)
    acc[...] = jnp.zeros_like(acc)
    split = slots // 256

    def pick(i, carry):
        where = pl.ds(pl.multiple_of(i * 256, 256), 256)
        into = pl.ds(pl.multiple_of(lax.rem(i, split) * 256, 256), 256)
        got = jnp.dot(vt[...], oh[:, where], preferred_element_type=F32)
        on = lax.broadcasted_iota(jnp.int32, (128, 256), 0) == ln[0:1, where]
        weight = wk[0:1, where]
        for l in range(n_l):
            value = jnp.where(on, got[l * 128:(l + 1) * 128], 0.0).reshape(16, 8, 256)
            acc[l, :, into] += jnp.sum(value, axis=0) * weight
        return carry

    lax.fori_loop(0, 4 * split, pick, 0)
    sb[lev, :, :] = jnp.zeros((8, slots), F32)
    for l in range(n_l):
        sb[lev, l:l + 1, :] = jnp.sum(acc[l], axis=0, keepdims=True) * er[l:l + 1, :]

    def level_copy(i, back=False):
        other = lax.rem(lev + (levs - i if back else i), levs)
        return pltpu.make_async_remote_copy(
            src_ref=sb.at[lev], dst_ref=sb.at[other if back else lev], send_sem=lev_send.at[other],
            recv_sem=lev_recv.at[other if back else lev], device_id={"lev": other},
        )

    for i in range(1, levs):
        level_copy(i).start()
    for i in range(1, levs):
        level_copy(i, back=True).wait_recv()
    coupled = [jnp.zeros((1, slots), F32) for _ in range(n_l)]
    for m in range(levs):
        for j in range(n_l):
            row = sb[m, j:j + 1, :]
            for l in range(n_l):
                coupled[l] = coupled[l] + corr[n_l * lev + l, n_l * m + j] * row
    for l in range(n_l):
        weighted = coupled[l] * er[l:l + 1, :]
        for k in range(4):
            where = pl.ds(k * slots, slots)
            value = weighted * wk[0:1, where]
            high = value.astype(BF16).astype(F32)
            sv[l, 0:1, where] = high
            sv[n_l + l, 0:1, where] = value - high

    def put(i, carry):
        rows = lax.broadcasted_iota(jnp.int32, (128, 4 * slots), 0)
        on = rows == ln[0:1, :]
        for g in range(2):
            xt[g * 128:(g + 1) * 128, :] = jnp.where(on, sv[2 * i + g, 0:1, :], 0.0).astype(BF16)
        adj[i, 0:qn, :] = lax.dot_general(oh[0:qn, :], xt[...], NT, preferred_element_type=F32)
        return carry

    lax.fori_loop(0, n_l, put, 0)
    for r in range(height):
        h = hb[DEPTH + r, 8:8 + n_t, :]
        for l in range(n_l):
            at = front + pitch * l
            low = n_l + l
            both = (
                adj[l // 2, r * n_t:(r + 1) * n_t, (l % 2) * 128:(l % 2 + 1) * 128]
                + adj[low // 2, r * n_t:(r + 1) * n_t, (low % 2) * 128:(low % 2 + 1) * 128]
            )
            u3[DEPTH + r, at:at + n_t, :] = h * both

    def start_second(chunk, carry):
        start_halo(1, chunk)
        return carry

    lax.fori_loop(0, chunks, start_second, 0)
    inner(u3)
    wait_halo(1, 0)
    nearest(u3)

    def arrived_again(chunk, carry):
        wait_halo(1, chunk)
        farther(u3, chunk)
        return carry

    lax.fori_loop(1, chunks, arrived_again, 0)

    def all_sent_again(chunk, carry):
        wait_sent(1, chunk)
        return carry

    lax.fori_loop(0, chunks, all_sent_again, 0)

    for r in range(height):
        part, here = r // 8, pl.ds(r % 8, n_t, stride=8)
        for l in range(n_l):
            at = front + pitch * l
            out[l, part, here, :] = rh[r, 0:n_t, :] * u2[DEPTH + r, at:at + n_t, :]

    every.wait_send()
    for i in range(1, levs):
        level_copy(i).wait_send()


def tiled(x, height, n_t):
    lead = x.shape[:-2]
    n = len(lead)
    x = x.reshape(lead + (height // 8, 8, n_t, 128))
    x = jnp.swapaxes(x, n + 1, n + 2)
    return x.reshape(lead + (height // 8, n_t * 8, 128))


def untiled(x, height, n_t):
    lead = x.shape[:-3]
    n = len(lead)
    x = x.reshape(lead + (height // 8, n_t, 8, 128))
    x = jnp.swapaxes(x, n + 1, n + 2)
    return x.reshape(lead + (height, n_t * 128))


def per_device(dims, control, land_sea, diffusivity, profile_counts, owner_tile, stencil_cells, stencil_weights,
               inverse_error, correlation_inverse):
    tiles, levs, n_l, height, n_t, stored = dims
    body = up_to((n_t + 1) * n_l, 8)
    hw = up_to(n_t, 8)
    rows = height + 2 * DEPTH
    qn, qp = height * n_t, up_to(height * n_t, 128)
    slots = RANKS * SRC
    vmem = pl.BlockSpec(memory_space=pltpu.VMEM)
    smem = pl.BlockSpec(memory_space=pltpu.SMEM)
    returned = pl.pallas_call(
        functools.partial(kernel, dims),
        out_shape=jax.ShapeDtypeStruct((n_l, height // 8, n_t * 8, 128), F32),
        in_specs=[vmem] * 7 + [smem] * 2,
        out_specs=vmem,
        scratch_shapes=[
            *[pltpu.VMEM((rows, body + 16, 128), F32) for _ in range(4)],
            pltpu.VMEM((rows, hw + 16, 128), F32),
            pltpu.VMEM((rows, body + 16, 128), F32),
            pltpu.VMEM((rows, body + 16, 128), F32),
            pltpu.VMEM((height, hw, 128), F32),
            pltpu.VMEM((SRC, 1, 256), F32),
            pltpu.VMEM((SRC, 1, 256), F32),
            pltpu.VMEM((2, 4 * slots), F32),
            pltpu.VMEM((1, 4 * slots), jnp.int32),
            pltpu.VMEM((8, slots), F32),
            pltpu.VMEM((n_l, 8, slots), F32),
            pltpu.VMEM((2 * qp, 4 * slots), BF16),
            pltpu.VMEM((n_l, qp, 128), F32),
            pltpu.VMEM((n_l * 128, 2 * qp), BF16),
            pltpu.VMEM((2 * n_l, 1, 4 * slots), F32),
            pltpu.VMEM((256, 4 * slots), BF16),
            pltpu.VMEM((n_l, up_to(qn, 8), 256), F32),
            pltpu.VMEM((levs, 8, slots), F32),
            pltpu.SemaphoreType.DMA((3, 2, DEPTH // CHUNK)),
            pltpu.SemaphoreType.DMA((3, 2, DEPTH // CHUNK)),
            pltpu.SemaphoreType.DMA((2,)),
            pltpu.SemaphoreType.DMA((2,)),
            pltpu.SemaphoreType.DMA((levs,)),
            pltpu.SemaphoreType.DMA((levs,)),
        ],
        compiler_params=pltpu.CompilerParams(
            collective_id=0, has_side_effects=True, vmem_limit_bytes=60 * 2**20
        ),
    )(
        tiled(control, height, n_t),
        tiled(land_sea, height, n_t),
        tiled(diffusivity, height, n_t),
        owner_tile.T,
        stencil_cells.T,
        stencil_weights.T,
        inverse_error.T,
        profile_counts,
        correlation_inverse,
    )
    return control + untiled(returned, height, n_t)


def solution(mesh):
    tiles, levs = mesh.shape["tile"], mesh.shape["lev"]

    def step(*args):
        n_l, height, columns = args[0].shape
        dims = (tiles, levs, n_l, height, columns // 128, args[4].shape[0])
        return per_device(dims, *args)

    return jax.shard_map(
        step,
        mesh=mesh,
        in_specs=(P("lev", "tile", None), P("tile", None), P("tile", None), P("tile"), P("tile", None), P("tile", None),
                  P("tile", None), P("tile", "lev"), P()),
        out_specs=P("lev", "tile", None),
        check_vma=False,
    )
```

```python
import functools

import jax
import jax.numpy as jnp
from jax import lax
from jax.experimental import pallas as pl
from jax.experimental.pallas import tpu as pltpu
from jax.sharding import PartitionSpec as P

ITERS = 10
DEPTH = ITERS
CHUNK = 2
SRC = 64
RANKS = 12
F32, BF16 = jnp.float32, jnp.bfloat16
NT = (((1,), (1,)), ((), ()))


def up_to(n, m):
    return -(-n // m) * m


def kernel(dims, ctrl, land, diff, owner, cells, weights, errors, counts, corr, out,
           u0, u1, u2, u3, hb, ca, cb, rh, sbuf, rbuf, wk, ln, er, acc, oh, vf, vt, sv, xt, adj, sb,
           halo_send, halo_recv, prof_send, prof_recv, lev_send, lev_recv):
    tiles, levs, n_l, height, n_t, stored = dims
    pitch, body, front = n_t + 1, up_to((n_t + 1) * n_l, 8), 8
    hw = up_to(n_t, 8)
    qn, qp = height * n_t, up_to(height * n_t, 128)
    slots = RANKS * SRC
    tile, lev = lax.axis_index("tile"), lax.axis_index("lev")
    lane = lax.broadcasted_iota(jnp.int32, (1, 128), 1)
    first, last = lane == 0, lane == 127

    barrier = pltpu.get_barrier_semaphore()

    def each_other(act):
        group = next(g for g in (7, 5, 3, 1) if (tiles - 1) % g == 0)

        def some(i, carry):
            for k in range(1, group + 1):
                act(lax.rem(tile + i * group + k, tiles))
            return carry

        lax.fori_loop(0, (tiles - 1) // group, some, 0)

    each_other(lambda t: pl.semaphore_signal(barrier, inc=1, device_id={"tile": t}))
    for i in range(1, levs):
        pl.semaphore_signal(barrier, inc=1, device_id={"lev": lax.rem(lev + i, levs)})

    rows_all = height + 2 * DEPTH

    def clear(r, carry):
        for u in (u0, u1, u2, u3):
            u[r, 0:front, :] = jnp.zeros((front, 128), F32)
            u[r, front + body:front + body + 8, :] = jnp.zeros((8, 128), F32)
        hb[r, 0:8, :] = jnp.zeros((8, 128), F32)
        hb[r, 8 + hw:16 + hw, :] = jnp.zeros((8, 128), F32)
        return carry

    lax.fori_loop(0, rows_all, clear, 0)

    def clear_halo(lo):
        def one(r, carry):
            for u in (u0, u3):
                u[r, front:front + body, :] = jnp.zeros((body, 128), F32)
            hb[r, 8:8 + hw, :] = jnp.zeros((hw, 128), F32)
            return carry

        lax.fori_loop(lo, lo + DEPTH, one, 0)

    @pl.when(tile == 0)
    def _():
        clear_halo(0)

    @pl.when(tile == tiles - 1)
    def _():
        clear_halo(DEPTH + height)

    for r in range(height):
        part, sub = r // 8, r % 8
        here = pl.ds(sub, n_t, stride=8)
        h = jnp.sqrt(land[part, here, :].astype(F32) * diff[part, here, :])
        hb[DEPTH + r, hw:8 + hw, :] = jnp.zeros((8, 128), F32)
        hb[DEPTH + r, 8:8 + n_t, :] = h
        rh[r, 0:n_t, :] = jnp.where(h > 0, 1.0 / h, 0.0)
        for l in range(n_l):
            at = front + pitch * l
            u0[DEPTH + r, at:at + n_t, :] = h * ctrl[l, part, here, :]
            for u in (u0, u3):
                end = at + pitch if l < n_l - 1 else front + body
                u[DEPTH + r, at + n_t:end, :] = jnp.zeros((end - at - n_t, 128), F32)

    pl.semaphore_wait(barrier, tiles - 1 + levs - 1)

    def halo(which, side, chunk, root=False):
        lo, n = chunk * CHUNK, CHUNK
        if side == 0:
            src, dst = DEPTH + lo, DEPTH + height + lo
        else:
            src, dst = height + DEPTH - lo - n, DEPTH - lo - n
        if root:
            a, b, which = hb.at[pl.ds(src, n), pl.ds(8, hw)], hb.at[pl.ds(dst, n), pl.ds(8, hw)], 2
        else:
            u = (u0, u3)[which]
            a, b = u.at[pl.ds(src, n), pl.ds(front, body)], u.at[pl.ds(dst, n), pl.ds(front, body)]
        return pltpu.make_async_remote_copy(
            src_ref=a, dst_ref=b, send_sem=halo_send.at[which, side, chunk], recv_sem=halo_recv.at[which, side, chunk],
            device_id={"tile": lax.rem(tile + (tiles - 1 if side == 0 else 1), tiles)},
        )

    def has(side):
        return tile > 0 if side == 0 else tile < tiles - 1

    def start_halo(which, chunk, root=False):
        for side in (0, 1):
            @pl.when(has(side))
            def _():
                halo(which, side, chunk, root).start()

    def wait_halo(which, chunk, root=False):
        for side in (0, 1):
            @pl.when(has(1 - side))
            def _():
                halo(which, side, chunk, root).wait_recv()

    def wait_sent(which, chunk, root=False):
        for side in (0, 1):
            @pl.when(has(side))
            def _():
                halo(which, side, chunk, root).wait_send()

    chunks = DEPTH // CHUNK

    def start_first(chunk, carry):
        start_halo(0, chunk, root=True)
        start_halo(0, chunk)
        return carry

    lax.fori_loop(0, chunks, start_first, 0)


    spot = lax.broadcasted_iota(jnp.int32, (1, stored), 1)
    living = spot < counts[0]
    is_owner = jnp.where(
        (lax.broadcasted_iota(jnp.int32, (SRC, stored), 0) == owner[...]) & living, 1.0, 0.0
    )
    mine = is_owner.astype(BF16)
    before = jnp.where(
        lax.broadcasted_iota(jnp.int32, (stored, stored), 0)
        < lax.broadcasted_iota(jnp.int32, (stored, stored), 1), 1.0, 0.0
    ).astype(BF16)
    ahead = jnp.dot(mine, before, preferred_element_type=F32)
    rank = jnp.sum(ahead * is_owner, axis=0, keepdims=True)
    data = jnp.concatenate(
        [cells[...].astype(F32), weights[...], errors[...], jnp.zeros((8 - n_l, stored), F32)], axis=0
    )
    spread_out = jnp.concatenate([jnp.where(rank == float(r), data, 0.0) for r in range(16)], axis=0)
    message = jnp.zeros((SRC, 256), F32)
    left = spread_out
    for _ in range(3):
        piece = left.astype(BF16)
        message += lax.dot_general(mine, piece, NT, preferred_element_type=F32)
        left = left - piece.astype(F32)
    sbuf[...] = message.reshape(SRC, 1, 256)

    def profile_copy(src, dst, to):
        return pltpu.make_async_remote_copy(
            src_ref=src, dst_ref=dst, send_sem=prof_send.at[0], recv_sem=prof_recv.at[0], device_id={"tile": to}
        )

    each_other(lambda t: profile_copy(sbuf.at[t], rbuf.at[tile], t).start())
    own = pltpu.make_async_copy(sbuf.at[tile], rbuf.at[tile], prof_recv.at[1])
    own.start()
    others = pl.ds(0, tiles - 1)
    every = profile_copy(sbuf.at[others], rbuf.at[others], lax.rem(tile + 1, tiles))

    def coefficients(lo, hi):
        def one(r, carry):
            h = hb[r, 8:8 + n_t, :]
            west = pltpu.roll(jnp.where(last, hb[r, 7:7 + n_t, :], h), 1, 1)
            east = pltpu.roll(jnp.where(first, hb[r, 9:9 + n_t, :], h), 127, 1)
            a = 1.0 - h * ((hb[r - 1, 8:8 + n_t, :] + hb[r + 1, 8:8 + n_t, :]) + (west + east))
            b = h * h
            for l in range(n_l):
                at = front + pitch * l
                end = at + pitch if l < n_l - 1 else front + body
                ca[r, at:at + n_t, :] = a
                cb[r, at:at + n_t, :] = b
                ca[r, at + n_t:end, :] = jnp.zeros((end - at - n_t, 128), F32)
                cb[r, at + n_t:end, :] = jnp.zeros((end - at - n_t, 128), F32)
            return carry

        lax.fori_loop(lo, hi, one, 0)

    mid = height // 2

    def sweep(src, dst, lo, n):
        def one(i, carry):
            for r in (DEPTH + lo + i, DEPTH + height - 1 - lo - i):
                made = []
                for j in range(front, front + body, 8):
                    here = pl.ds(j, 8)
                    c = src[r, here, :]
                    west = pltpu.roll(jnp.where(last, src[r, j - 1:j + 7, :], c), 1, 1)
                    east = pltpu.roll(jnp.where(first, src[r, j + 1:j + 9, :], c), 127, 1)
                    around = (src[r - 1, here, :] + src[r + 1, here, :]) + (west + east)
                    made.append(ca[r, here, :] * c + cb[r, here, :] * around)
                for j, value in zip(range(front, front + body, 8), made):
                    dst[r, pl.ds(j, 8), :] = value
            return carry

        lax.fori_loop(0, n, one, 0)

    def steps(begin, reach, total):
        sweep(begin, u1, *reach(1))

        def two(t, carry):
            sweep(u1, u2, *reach(2 * t))
            sweep(u2, u1, *reach(2 * t + 1))
            return carry

        lax.fori_loop(1, (total + 1) // 2, two, 0)
        if total % 2 == 0:
            sweep(u1, u2, *reach(total))

    def inner(begin):
        steps(begin, lambda s: (s, mid - s), mid - 1)

    def nearest(begin):
        steps(begin, lambda s: (s - CHUNK, jnp.minimum(CHUNK, mid + CHUNK - s)), ITERS)

    def both_ends(src, dst, lo):
        for top in (DEPTH + lo, DEPTH + height - lo - CHUNK):
            for half in range(front, front + body, body // 2):
                made = []
                for j in range(half, half + body // 2, 8):
                    here = pl.ds(j, 8)
                    c = [src[top + i, here, :] for i in range(-1, CHUNK + 1)]
                    for i in range(CHUNK):
                        r, own = top + i, c[i + 1]
                        west = pltpu.roll(jnp.where(last, src[r, j - 1:j + 7, :], own), 1, 1)
                        east = pltpu.roll(jnp.where(first, src[r, j + 1:j + 9, :], own), 127, 1)
                        around = (c[i] + c[i + 2]) + (west + east)
                        made.append((r, here, ca[r, here, :] * own + cb[r, here, :] * around))
                for r, here, value in made:
                    dst[r, here, :] = value

    def farther(begin, chunk):
        lo = -CHUNK * (chunk + 1)
        both_ends(begin, u1, lo + 1)

        def two(t, carry):
            both_ends(u1, u2, lo + 2 * t)
            both_ends(u2, u1, lo + 2 * t + 1)
            return carry

        lax.fori_loop(1, ITERS // 2, two, 0)
        both_ends(u1, u2, lo + ITERS)

    coefficients(DEPTH + 1, DEPTH + height - 1)
    inner(u0)

    def more_roots(chunk):
        wait_halo(0, chunk, root=True)
        coefficients(DEPTH - CHUNK * chunk - 1, DEPTH - CHUNK * chunk + 1)
        coefficients(DEPTH + height + CHUNK * chunk - 1, DEPTH + height + CHUNK * chunk + 1)
        wait_halo(0, chunk)

    more_roots(0)
    nearest(u0)

    def arrived(chunk, carry):
        more_roots(chunk)
        farther(u0, chunk)
        return carry

    lax.fori_loop(1, chunks, arrived, 0)

    def all_sent(chunk, carry):
        wait_sent(0, chunk, root=True)
        wait_sent(0, chunk)
        return carry

    lax.fori_loop(0, chunks, all_sent, 0)

    every.wait_recv()
    own.wait()
    heard = jnp.concatenate([rbuf[...].reshape(SRC, 256), jnp.zeros((128 - SRC, 256), F32)], axis=0)
    turned = jnp.transpose(heard)
    for pair in range(RANKS // 2):
        both = turned[32 * pair:32 * pair + 16] + pltpu.roll(turned[32 * pair + 16:32 * pair + 32], SRC, 1)
        for k in range(4):
            where = pl.ds(k * slots + pair * 128, 128)
            cell = both[k:k + 1].astype(jnp.int32)
            wk[1:2, where] = (cell >> 7).astype(F32)
            ln[0:1, where] = cell & 127
            wk[0:1, where] = both[4 + k:5 + k]
        er[0:8, pl.ds(pair * 128, 128)] = both[8:16]

    def one_hots(i, carry):
        rows = lax.broadcasted_iota(jnp.int32, (128, 4 * slots), 0) + i * 128
        hot = jnp.where(rows == wk[1:2, :].astype(jnp.int32), 1.0, 0.0).astype(BF16)
        oh[pl.ds(pl.multiple_of(i * 128, 128), 128), :] = hot
        oh[pl.ds(pl.multiple_of(qp + i * 128, 128), 128), :] = hot
        return carry

    lax.fori_loop(0, qp // 128, one_hots, 0)

    for l in range(n_l):
        at = front + pitch * l
        for r in range(height):
            vf[l, r * n_t:(r + 1) * n_t, :] = rh[r, 0:n_t, :] * u2[DEPTH + r, at:at + n_t, :]
        if qp > qn:
            vf[l, qn:qp, :] = jnp.zeros((qp - qn, 128), F32)

    def turn(l, carry):
        here = pl.ds(pl.multiple_of(l * 128, 128), 128)
        value = jnp.transpose(vf[l, :, :])
        high = value.astype(BF16)
        vt[here, 0:qp] = high
        vt[here, qp:2 * qp] = (value - high.astype(F32)).astype(BF16)
        return carry

    lax.fori_loop(0, n_l, turn, 0)
    acc[...] = jnp.zeros_like(acc)
    split = slots // 256

    def pick(i, carry):
        where = pl.ds(pl.multiple_of(i * 256, 256), 256)
        into = pl.ds(pl.multiple_of(lax.rem(i, split) * 256, 256), 256)
        got = jnp.dot(vt[...], oh[:, where], preferred_element_type=F32)
        on = lax.broadcasted_iota(jnp.int32, (128, 256), 0) == ln[0:1, where]
        weight = wk[0:1, where]
        for l in range(n_l):
            value = jnp.where(on, got[l * 128:(l + 1) * 128], 0.0).reshape(16, 8, 256)
            acc[l, :, into] += jnp.sum(value, axis=0) * weight
        return carry

    lax.fori_loop(0, 4 * split, pick, 0)
    sb[lev, :, :] = jnp.zeros((8, slots), F32)
    for l in range(n_l):
        sb[lev, l:l + 1, :] = jnp.sum(acc[l], axis=0, keepdims=True) * er[l:l + 1, :]

    def level_copy(i, back=False):
        other = lax.rem(lev + (levs - i if back else i), levs)
        return pltpu.make_async_remote_copy(
            src_ref=sb.at[lev], dst_ref=sb.at[other if back else lev], send_sem=lev_send.at[other],
            recv_sem=lev_recv.at[other if back else lev], device_id={"lev": other},
        )

    for i in range(1, levs):
        level_copy(i).start()
    for i in range(1, levs):
        level_copy(i, back=True).wait_recv()
    coupled = [jnp.zeros((1, slots), F32) for _ in range(n_l)]
    for m in range(levs):
        for j in range(n_l):
            row = sb[m, j:j + 1, :]
            for l in range(n_l):
                coupled[l] = coupled[l] + corr[n_l * lev + l, n_l * m + j] * row
    for l in range(n_l):
        weighted = coupled[l] * er[l:l + 1, :]
        for k in range(4):
            where = pl.ds(k * slots, slots)
            value = weighted * wk[0:1, where]
            high = value.astype(BF16).astype(F32)
            sv[l, 0:1, where] = high
            sv[n_l + l, 0:1, where] = value - high

    def put(i, carry):
        rows = lax.broadcasted_iota(jnp.int32, (128, 4 * slots), 0)
        on = rows == ln[0:1, :]
        for g in range(2):
            xt[g * 128:(g + 1) * 128, :] = jnp.where(on, sv[2 * i + g, 0:1, :], 0.0).astype(BF16)
        adj[i, 0:qn, :] = lax.dot_general(oh[0:qn, :], xt[...], NT, preferred_element_type=F32)
        return carry

    lax.fori_loop(0, n_l, put, 0)
    for r in range(height):
        h = hb[DEPTH + r, 8:8 + n_t, :]
        for l in range(n_l):
            at = front + pitch * l
            low = n_l + l
            both = (
                adj[l // 2, r * n_t:(r + 1) * n_t, (l % 2) * 128:(l % 2 + 1) * 128]
                + adj[low // 2, r * n_t:(r + 1) * n_t, (low % 2) * 128:(low % 2 + 1) * 128]
            )
            u3[DEPTH + r, at:at + n_t, :] = h * both

    def start_second(chunk, carry):
        start_halo(1, chunk)
        return carry

    lax.fori_loop(0, chunks, start_second, 0)
    inner(u3)
    wait_halo(1, 0)
    nearest(u3)

    def arrived_again(chunk, carry):
        wait_halo(1, chunk)
        farther(u3, chunk)
        return carry

    lax.fori_loop(1, chunks, arrived_again, 0)

    def all_sent_again(chunk, carry):
        wait_sent(1, chunk)
        return carry

    lax.fori_loop(0, chunks, all_sent_again, 0)

    for r in range(height):
        part, here = r // 8, pl.ds(r % 8, n_t, stride=8)
        for l in range(n_l):
            at = front + pitch * l
            out[l, part, here, :] = rh[r, 0:n_t, :] * u2[DEPTH + r, at:at + n_t, :]

    every.wait_send()
    for i in range(1, levs):
        level_copy(i).wait_send()


def tiled(x, height, n_t):
    lead = x.shape[:-2]
    n = len(lead)
    x = x.reshape(lead + (height // 8, 8, n_t, 128))
    x = jnp.swapaxes(x, n + 1, n + 2)
    return x.reshape(lead + (height // 8, n_t * 8, 128))


def untiled(x, height, n_t):
    lead = x.shape[:-3]
    n = len(lead)
    x = x.reshape(lead + (height // 8, n_t, 8, 128))
    x = jnp.swapaxes(x, n + 1, n + 2)
    return x.reshape(lead + (height, n_t * 128))


def per_device(dims, control, land_sea, diffusivity, profile_counts, owner_tile, stencil_cells, stencil_weights,
               inverse_error, correlation_inverse):
    tiles, levs, n_l, height, n_t, stored = dims
    body = up_to((n_t + 1) * n_l, 8)
    hw = up_to(n_t, 8)
    rows = height + 2 * DEPTH
    qn, qp = height * n_t, up_to(height * n_t, 128)
    slots = RANKS * SRC
    vmem = pl.BlockSpec(memory_space=pltpu.VMEM)
    smem = pl.BlockSpec(memory_space=pltpu.SMEM)
    returned = pl.pallas_call(
        functools.partial(kernel, dims),
        out_shape=jax.ShapeDtypeStruct((n_l, height // 8, n_t * 8, 128), F32),
        in_specs=[vmem] * 7 + [smem] * 2,
        out_specs=vmem,
        scratch_shapes=[
            *[pltpu.VMEM((rows, body + 16, 128), F32) for _ in range(4)],
            pltpu.VMEM((rows, hw + 16, 128), F32),
            pltpu.VMEM((rows, body + 16, 128), F32),
            pltpu.VMEM((rows, body + 16, 128), F32),
            pltpu.VMEM((height, hw, 128), F32),
            pltpu.VMEM((SRC, 1, 256), F32),
            pltpu.VMEM((SRC, 1, 256), F32),
            pltpu.VMEM((2, 4 * slots), F32),
            pltpu.VMEM((1, 4 * slots), jnp.int32),
            pltpu.VMEM((8, slots), F32),
            pltpu.VMEM((n_l, 8, slots), F32),
            pltpu.VMEM((2 * qp, 4 * slots), BF16),
            pltpu.VMEM((n_l, qp, 128), F32),
            pltpu.VMEM((n_l * 128, 2 * qp), BF16),
            pltpu.VMEM((2 * n_l, 1, 4 * slots), F32),
            pltpu.VMEM((256, 4 * slots), BF16),
            pltpu.VMEM((n_l, up_to(qn, 8), 256), F32),
            pltpu.VMEM((levs, 8, slots), F32),
            pltpu.SemaphoreType.DMA((3, 2, DEPTH // CHUNK)),
            pltpu.SemaphoreType.DMA((3, 2, DEPTH // CHUNK)),
            pltpu.SemaphoreType.DMA((2,)),
            pltpu.SemaphoreType.DMA((2,)),
            pltpu.SemaphoreType.DMA((levs,)),
            pltpu.SemaphoreType.DMA((levs,)),
        ],
        compiler_params=pltpu.CompilerParams(
            collective_id=0, has_side_effects=True, vmem_limit_bytes=60 * 2**20
        ),
    )(
        tiled(control, height, n_t),
        tiled(land_sea, height, n_t),
        tiled(diffusivity, height, n_t),
        owner_tile.T,
        stencil_cells.T,
        stencil_weights.T,
        inverse_error.T,
        profile_counts,
        correlation_inverse,
    )
    return control + untiled(returned, height, n_t)


def solution(mesh):
    tiles, levs = mesh.shape["tile"], mesh.shape["lev"]

    def step(*args):
        n_l, height, columns = args[0].shape
        dims = (tiles, levs, n_l, height, columns // 128, args[4].shape[0])
        return per_device(dims, *args)

    return jax.shard_map(
        step,
        mesh=mesh,
        in_specs=(P("lev", "tile", None), P("tile", None), P("tile", None), P("tile"), P("tile", None), P("tile", None),
                  P("tile", None), P("tile", "lev"), P()),
        out_specs=P("lev", "tile", None),
        check_vma=False,
    )
```
